128 devices in a mesh: gx: 4 (over z_hi, core), gy: 4 (over x), gz: 8 (over z_lo, y).
Axes of the slice: x: 4, y: 4, z: 4 (z_hi: 2, z_lo: 2; z = z_hi * 2 + z_lo), core: 2. Of those that a mesh axis runs over, the one named last changes fastest.
Arguments:
- positions: float32 [16, 16, 8, 96], P('gx', 'gy', 'gz'), as said below
- species: int32 [16, 16, 8, 32], P('gx', 'gy', 'gz'), may hold values from 0 to 1
- counts: int32 [16, 16, 8], P('gx', 'gy', 'gz'), may hold values from 2 to 32, as said below
- neighbours: int32 [16, 16, 8, 512], P('gx', 'gy', 'gz'), may hold values from 0 to 863, as said below
- w_radial: float32 [64, 8], replicated, may hold values from -2 to 2
- emb_center: float32 [64, 2], replicated, may hold values from -6 to 6
- emb_nbr: float32 [64, 2], replicated, may hold values from -6 to 6
- w_first: float32 [64, 128], replicated, may hold values from -0.5 to 0.5
- w_second: float32 [64, 192], replicated, may hold values from -0.4375 to 0.4375
- w_out: float32 [64], replicated, may hold values from -0.75 to 0.75
Outputs:
- atom_out: float32 [16, 16, 8, 128], P('gx', 'gy', 'gz')
The draws below stay inside these ranges and needn't reach their ends.
Inputs may be any that keep to these rules, and one draw needn't show every extreme that they name: A tile's first counts slots are occupied; one tile is full and one holds 2. Entries a * 16 to a * 16 + 15 of a tile are distinct neighbours of slot a; none names the slot itself. `positions`: occupied or not, two distinct atom slots lie 1.4 or more apart.
All inputs are finite; a program needn't handle non-finite values.
Results may differ from the reference program's by a relative error of at most 0.0003.
Values sent between devices are 32-bit elements; how exact they have to be, the bound alone decides.
A program may use at most 64 MiB of HBM per device.

```python
import math
import jax
import jax.numpy as jnp
import numpy as np
from jax import lax

CH = 64
NB = 8
SPECIES = 2
SLOTS = 32
NBR = 16
EDGES = 512
TX = 4
TY = 4
TZ = 1
NXT = 16
NYT = 16
NZT = 8


def candidate_steps():
    listed = [(step_x, step_y, step_z) for step_x in range(-2, 3) for step_y in range(-2, 3) for step_z in range(-1, 2) if (step_x, step_y, step_z) != (0, 0, 0)]
    return np.array(listed, dtype=np.int32).T


def draw_positions(key, part):
    key = jax.random.fold_in(key, 11)
    slot_index = jnp.arange(SLOTS)
    lattice = jnp.stack([2.0 * (slot_index // 8) + 1.0, 2.0 * (slot_index // 2 % 4) + 1.0, 4.0 * (slot_index % 2) + 2.0], axis=1)
    jitter = jax.random.uniform(key, (NXT, NYT, NZT, SLOTS, 3), jnp.float32, -0.3, 0.3)
    return (lattice + jitter).reshape(NXT, NYT, NZT, SLOTS * 3)


def draw_counts(key, part):
    key = jax.random.fold_in(key, 12)
    dense_key, fill_key, sparse_key = jax.random.split(key, 3)
    dense_tiles = jax.random.randint(dense_key, (NXT, NYT, NZT), 0, 3) == 0
    full_counts = SLOTS - jax.random.randint(fill_key, (NXT, NYT, NZT), 0, 4)
    sparse_counts = jax.random.randint(sparse_key, (NXT, NYT, NZT), 2, SLOTS // 2)
    result = jnp.where(dense_tiles, full_counts, sparse_counts)
    return result.at[0, 0, 0].set(SLOTS).at[-1, -1, -1].set(2)


def draw_neighbours(key, part):
    key = jax.random.fold_in(key, 13)
    candidates = jnp.asarray(candidate_steps())
    candidate_total = candidates.shape[1]
    scores = jax.random.randint(key, (NXT * NYT * NZT, SLOTS, candidate_total), 0, 1 << 20) * 128 + jnp.arange(candidate_total, dtype=jnp.int32)
    picked = jnp.argsort(scores, axis=2)[:, :, :NBR]
    slot_index = jnp.arange(SLOTS, dtype=jnp.int32)
    reach_x = (slot_index // 8)[:, None] + candidates[0][picked]
    reach_y = (slot_index // 2 % 4)[:, None] + candidates[1][picked]
    reach_z = (slot_index % 2)[:, None] + candidates[2][picked]
    offset = (reach_x // 4 + 1) * 9 + (reach_y // 4 + 1) * 3 + (reach_z // 2 + 1)
    target = reach_x % 4 * 8 + reach_y % 4 * 2 + reach_z % 2
    return (offset * SLOTS + target).reshape(NXT, NYT, NZT, EDGES)


def set_ends(values, rng, smallest, top_value):
    extent = values.shape
    place = [jax.random.randint(jax.random.fold_in(rng, axis), (), 0, extent[axis]) for axis in range(len(extent))]
    values = values.at[tuple(place)].set(smallest)
    longest = extent.index(max(extent))
    place[longest] = (place[longest] + 1) % extent[longest]
    return values.at[tuple(place)].set(top_value)


def scatter_about(stream_key, shape, width, most, kind=jnp.bfloat16):
    drawn = jax.random.normal(stream_key, shape, jnp.float32) * width
    return jnp.minimum(jnp.maximum(drawn, -most), most).astype(kind)


def setup_inputs(seed: int = 0) -> dict:
    seeds = jax.random.split(jax.random.key(seed), 11)
    return {
        "positions": draw_positions(jax.random.fold_in(seeds[10], 71), 0),
        "species": set_ends(jax.random.randint(seeds[1], (NXT, NYT, NZT, SLOTS), 0, SPECIES), jax.random.fold_in(seeds[1], 1), 0, SPECIES - 1).astype(jnp.int32),
        "counts": draw_counts(jax.random.fold_in(seeds[10], 71), 0),
        "neighbours": draw_neighbours(jax.random.fold_in(seeds[10], 71), 0),
        "w_radial": scatter_about(seeds[4], (CH, NB), NB ** -0.5, 2.0, jnp.float32),
        "emb_center": scatter_about(seeds[5], (CH, SPECIES), 1.0, 6.0, jnp.float32),
        "emb_nbr": scatter_about(seeds[6], (CH, SPECIES), 1.0, 6.0, jnp.float32),
        "w_first": scatter_about(seeds[7], (CH, 2 * CH), (2 * CH) ** -0.5, 0.5, jnp.float32),
        "w_second": scatter_about(seeds[8], (CH, 3 * CH), (3 * CH) ** -0.5, 0.4375, jnp.float32),
        "w_out": scatter_about(seeds[9], (CH,), CH ** -0.5, 0.75, jnp.float32),
    }


cutoff_len = 5.0
tile_len = 8.0

def matmul(left, right):
    return jnp.dot(left, right, precision=lax.Precision.HIGHEST, preferred_element_type=jnp.float32)

def envelope(distance):
    scaled = distance / cutoff_len
    polynomial = 1.0 - 28.0 * scaled ** 6 + 48.0 * scaled ** 7 - 21.0 * scaled ** 8
    return jnp.where(scaled < 1.0, polynomial, 0.0)

def center_sum(values):
    return lax.optimization_barrier(jnp.sum(values.reshape(values.shape[0], -1, NBR), axis=2)) * NBR ** (-0.5)

def phase_first(vectors, live_mask, own_hot, nbr_hot, w_radial, emb_center, emb_nbr, w_first):
    distance = jnp.sqrt(lax.optimization_barrier(jnp.sum(vectors * vectors, axis=0)))
    weight = envelope(distance) * live_mask
    orders = jnp.arange(1, w_radial.shape[1] + 1).astype(jnp.float32)
    radial_basis = jnp.sin(orders[:, None] * (math.pi / cutoff_len) * distance[None, :]) / distance[None, :]
    initial = matmul(w_radial, radial_basis) + matmul(emb_center, own_hot) + matmul(emb_nbr, nbr_hot)
    edge_first = jax.nn.silu(initial) * weight[None, :]
    channels = edge_first.shape[0]
    env_spread = jnp.repeat(center_sum(edge_first), NBR, axis=1)
    update = matmul(w_first[:, :channels], edge_first) + matmul(w_first[:, channels:], env_spread)
    second = edge_first + weight[None, :] * jax.nn.silu(update)
    atom_state = center_sum(weight[None, :] * second)
    return (second, atom_state, weight)

def phase_second(second, weight, atom_state, state_nbr, w_second, w_out):
    channels = second.shape[0]
    own_spread = jnp.repeat(atom_state, NBR, axis=1)
    mixture = matmul(w_second[:, :channels], second) + matmul(w_second[:, channels:2 * channels], own_spread)
    mixture = mixture + matmul(w_second[:, 2 * channels:], state_nbr)
    edge_third = second + weight[None, :] * jax.nn.silu(mixture)
    per_edge = weight * matmul(w_out[None, :], edge_third)[0]
    return lax.optimization_barrier(jnp.sum(per_edge.reshape(-1, NBR), axis=1))

def reference(positions, species, counts, neighbours, w_radial, emb_center, emb_nbr, w_first, w_second, w_out):
    tiles_x, tiles_y, tiles_z = counts.shape
    slot_count = species.shape[3]
    tile_total = tiles_x * tiles_y * tiles_z
    edge_count = neighbours.shape[3]
    channels = w_out.shape[0]
    group_size = TX * TY * TZ
    blocks = tile_total // group_size
    pos_flat = positions.reshape(tile_total * slot_count, 3)
    slot_ids = jnp.arange(slot_count, dtype=jnp.int32)
    labels = jnp.where(slot_ids[None, :] < counts.reshape(tile_total, 1), species.reshape(tile_total, slot_count), -1).reshape(-1)
    occupied = (labels >= 0).astype(jnp.float32)
    species_ids = jnp.arange(emb_center.shape[1], dtype=jnp.int32)
    one_hot = (labels[None, :] == species_ids[:, None]).astype(jnp.float32)
    nbr_flat = neighbours.reshape(tile_total, edge_count)
    atom_block = group_size * slot_count

    def edge_data(block_id):
        tile_ids = block_id * group_size + jnp.arange(group_size, dtype=jnp.int32)
        nearby = lax.dynamic_slice_in_dim(nbr_flat, block_id * group_size, group_size, 0)
        coord_x = tile_ids // (tiles_y * tiles_z)
        coord_y = tile_ids // tiles_z % tiles_y
        coord_z = tile_ids % tiles_z
        which = nearby // slot_count
        step_x = which // 9 - 1
        step_y = which // 3 % 3 - 1
        step_z = which % 3 - 1
        nbr_tile = ((coord_x[:, None] + step_x) % tiles_x * tiles_y + (coord_y[:, None] + step_y) % tiles_y) * tiles_z + (coord_z[:, None] + step_z) % tiles_z
        nbr_atom = (nbr_tile * slot_count + nearby % slot_count).reshape(-1)
        center_atom = (tile_ids[:, None] * slot_count + (jnp.arange(edge_count, dtype=jnp.int32) // NBR)[None, :]).reshape(-1)
        offsets = jnp.stack([step_x, step_y, step_z]).reshape(3, -1).astype(jnp.float32) * tile_len
        vectors = offsets + pos_flat[nbr_atom].T - pos_flat[center_atom].T
        live_mask = occupied[center_atom] * occupied[nbr_atom]
        return (vectors, live_mask, one_hot[:, center_atom], one_hot[:, nbr_atom], nbr_atom, center_atom)

    def first_pass(block_id):
        vectors, live_mask, own_hot, nbr_hot, nbr_atom, center_atom = edge_data(block_id)
        second, atom_state, weight = phase_first(vectors, live_mask, own_hot, nbr_hot, w_radial, emb_center, emb_nbr, w_first)
        return atom_state.T
    block_ids = jnp.arange(blocks, dtype=jnp.int32)
    states = lax.map(first_pass, block_ids).reshape(tile_total * slot_count, channels)

    def second_pass(totals, block_id):
        vectors, live_mask, own_hot, nbr_hot, nbr_atom, center_atom = edge_data(block_id)
        second, atom_state, weight = phase_first(vectors, live_mask, own_hot, nbr_hot, w_radial, emb_center, emb_nbr, w_first)

        def energy_of(state_nbr):
            return phase_second(second, weight, atom_state, state_nbr, w_second, w_out)
        energy, pullback = jax.vjp(energy_of, states[nbr_atom].T)
        grad_nbr, = pullback(jnp.ones_like(energy))
        return (totals.at[nbr_atom].add(grad_nbr.T), None)
    returned, unused = lax.scan(second_pass, jnp.zeros((tile_total * slot_count, channels), jnp.float32), block_ids)

    def third_pass(totals, block_id):
        vectors, live_mask, own_hot, nbr_hot, nbr_atom, center_atom = edge_data(block_id)
        near_state = states[nbr_atom].T

        def combined(vector_in):
            second, atom_state, weight = phase_first(vector_in, live_mask, own_hot, nbr_hot, w_radial, emb_center, emb_nbr, w_first)
            return (phase_second(second, weight, atom_state, near_state, w_second, w_out), atom_state)
        (energy, atom_state), pullback = jax.vjp(combined, vectors)
        outside = lax.dynamic_slice_in_dim(returned, block_id * atom_block, atom_block, 0).T
        grad_vec, = pullback((jnp.ones_like(energy), outside))
        totals = totals.at[center_atom].add(grad_vec.T).at[nbr_atom].add(-grad_vec.T)
        return (totals, energy)
    forces, energies = lax.scan(third_pass, jnp.zeros((tile_total * slot_count, 3), jnp.float32), block_ids)
    result = jnp.concatenate([forces.reshape(tile_total, slot_count, 3), energies.reshape(tile_total, slot_count, 1)], axis=2)
    return result.reshape(tiles_x, tiles_y, tiles_z, slot_count * 4)
```

```python
import functools
import math

import jax
import jax.numpy as jnp
from jax import lax
from jax.experimental import pallas as pl
from jax.experimental.pallas import tpu as pltpu
from jax.sharding import PartitionSpec as P

F32 = jnp.float32
BF16 = jnp.bfloat16
I32 = jnp.int32

CUT = 5.0
TILE = 8.0
CH = 64
NBR = 16
SLOTS = 32
EDGES = 512
TX = 4
TY = 4
TILES = TX * TY
LANES = 128
TARGETS = 27 * SLOTS

DIRS = [
    (dx, dy, dz)
    for dz in (-1, 1, 0)
    for dx in (-1, 0, 1)
    for dy in (-1, 0, 1)
    if (dx, dy, dz) != (0, 0, 0)
]


def edge_of(step, count):
    if step == 0:
        return pl.ds(1, count)
    return pl.ds(count if step > 0 else 1, 1)


def ghost_of(step, count):
    if step == 0:
        return pl.ds(1, count)
    return pl.ds(count + 1 if step > 0 else 0, 1)


def device_at(step):
    names = ("gx", "gy", "gz")
    place = []
    for name, move in zip(names, step):
        size = lax.axis_size(name)
        place.append(lax.rem(lax.axis_index(name) + (move + size), size))
    return tuple(place)


def outward(buf, sems, base):
    send, recv = sems
    made = []
    for index, (dx, dy, dz) in enumerate(DIRS):
        made.append(
            pltpu.make_async_remote_copy(
                src_ref=buf.at[1, edge_of(dx, TX), edge_of(dy, TY)],
                dst_ref=buf.at[1 - dz, ghost_of(-dx, TX), ghost_of(-dy, TY)],
                send_sem=send.at[base + index],
                recv_sem=recv.at[base + index],
                device_id=device_at((dx, dy, dz)),
                device_id_type=pl.DeviceIdType.MESH,
            )
        )
    return made


def homeward(source, target, sems, base):
    send, recv = sems
    made = []
    for index, (dx, dy, dz) in enumerate(DIRS):
        place = (1 + dz, ghost_of(dx, TX), ghost_of(dy, TY))
        made.append(
            pltpu.make_async_remote_copy(
                src_ref=source.at[place],
                dst_ref=target.at[place],
                send_sem=send.at[base + index],
                recv_sem=recv.at[base + index],
                device_id=device_at((dx, dy, dz)),
                device_id_type=pl.DeviceIdType.MESH,
            )
        )
    return made


def shares(x, y):
    found = []
    for dx, dy, dz in DIRS:
        if dx != 0 and x != (0 if dx > 0 else TX - 1):
            continue
        if dy != 0 and y != (0 if dy > 0 else TY - 1):
            continue
        px = x + 1 if dx == 0 else (TX + 1 if dx > 0 else 0)
        py = y + 1 if dy == 0 else (TY + 1 if dy > 0 else 0)
        found.append((1 + dz, px, py))
    return found


def halves(x):
    high = x.astype(BF16)
    low = (x - high.astype(F32)).astype(BF16)
    return high, low


def stack3(x):
    high, low = halves(x)
    return jnp.concatenate([high, low, high], axis=0)


def weight3(w):
    high, low = halves(w)
    return jnp.concatenate([high, high, low], axis=1)


def dot(left, right):
    return lax.dot_general(
        left, right, (((1,), (0,)), ((), ())), preferred_element_type=F32
    )


def dot_t(left, right):
    return lax.dot_general(
        left, right, (((1,), (1,)), ((), ())), preferred_element_type=F32
    )


def exact_dot(left, right):
    return lax.dot_general(
        left,
        right,
        (((1,), (0,)), ((), ())),
        preferred_element_type=F32,
        precision=lax.Precision.HIGHEST,
    )


def over_edges(x):
    total = (x[:, 0:128] + x[:, 128:256]) + (x[:, 256:384] + x[:, 384:512])
    total = total + pltpu.roll(total, 64, 1)
    return total + pltpu.roll(total, 32, 1)


def spread(x):
    return jnp.concatenate([x, x, x, x], axis=1)


def polynomial(x, coefficients):
    total = jnp.full_like(x, coefficients[-1])
    for value in reversed(coefficients[:-1]):
        total = total * x + value
    return total


SIN = [(-1.0) ** i * math.pi ** (2 * i + 1) / math.factorial(2 * i + 1) for i in range(7)]
COS = [(-1.0) ** i * math.pi ** (2 * i) / math.factorial(2 * i) for i in range(8)]


def iota(shape, dim):
    return lax.broadcasted_iota(I32, shape, dim)


def kernel(
    pos_ref, spec_ref, count_ref, nbr_ref, wr_ref, ec_ref, en_ref, w1_ref, w2_ref, wo_ref,
    out_ref,
    pos_grid, own_cols, pos_cols, c9_s, loc_s, o_s, b_s,
    onehot, wf_s, w1a_s, w1b_s, w2bc_s, w2a_s, w2at_s, w2bt_s, w2ct_s, w1at_s, w1bt_s, wrt_s, wo_s,
    silu1, slope1, silu2, slope2, second_s, mix_s, back_s,
    weight_s, dweight_s, dwacc_s, unit_s, dradial_s, q_s, sum_s,
    p_grid, p_cols, acc, g_send, g_recv, f_send, f_recv, result_s,
    send_sem, recv_sem,
):
    sems = (send_sem, recv_sem)
    barrier = pltpu.get_barrier_semaphore()
    for step in DIRS:
        pl.semaphore_signal(
            barrier, inc=1, device_id=device_at(step), device_id_type=pl.DeviceIdType.MESH
        )

    rows, cols = iota((96, LANES), 0), iota((96, LANES), 1)
    place = jnp.where(cols < 96, jnp.where(rows == (cols % 32) * 3 + cols // 32, 1.0, 0.0), 0.0)
    labels = jnp.where(iota((TILES, SLOTS), 1) < count_ref[...], spec_ref[...], -1).astype(F32)
    shift = jnp.where(iota((SLOTS, LANES), 1) == iota((SLOTS, LANES), 0) + 96, 1.0, 0.0).astype(F32)
    packed = exact_dot(pos_ref[...], place) + exact_dot(labels, shift)
    for t in range(TILES):
        pos_grid[1, 1 + t // TY, 1 + t % TY] = packed[t : t + 1]

    pl.semaphore_wait(barrier, len(DIRS))
    copies = outward(pos_grid, sems, 0)
    for copy in copies:
        copy.start()

    entry = nbr_ref[...]
    order = jnp.where(
        iota((EDGES, EDGES), 0) == (iota((EDGES, EDGES), 1) % 32) * 16 + iota((EDGES, EDGES), 1) // 32,
        1.0,
        0.0,
    ).astype(BF16)
    o_new = dot((entry // 32).astype(F32).astype(BF16), order).astype(I32)
    b_new = dot((entry % 32).astype(F32).astype(BF16), order).astype(I32)
    c9_new = o_new // 3
    loc_new = (o_new % 3) * 32 + b_new
    for t in range(TILES):
        o_s[t] = o_new[t : t + 1]
        b_s[t] = b_new[t : t + 1]
        c9_s[t] = c9_new[t : t + 1]
        loc_s[t] = loc_new[t : t + 1]

    half = 0.5
    features = jnp.concatenate(
        [wr_ref[...], ec_ref[...], en_ref[...], jnp.zeros((CH, 4), F32)], axis=1
    )
    wf_s[...] = weight3(features * half)
    w1 = w1_ref[...]
    w2 = w2_ref[...]
    w1a, w1b = w1[:, :CH], w1[:, CH:]
    w2a, w2b, w2c = w2[:, :CH], w2[:, CH : 2 * CH], w2[:, 2 * CH :]
    w1a_s[...] = weight3(w1a * half)
    w1b_s[...] = weight3(w1b * half)
    w2bc_s[...] = weight3(jnp.concatenate([w2b, w2c], axis=0) * half)
    w2a_s[...] = weight3(w2a * half)
    w2at_s[...] = weight3(w2a.T)
    w2bt_s[...] = weight3(w2b.T)
    w2ct_s[...] = w2c.T
    w1at_s[...] = weight3(w1a.T)
    w1bt_s[...] = weight3(w1b.T)
    wrt_s[...] = weight3(jnp.concatenate([wr_ref[...], jnp.zeros((CH, 8), F32)], axis=1).T)
    wo_s[...] = jnp.broadcast_to(
        jnp.broadcast_to(wo_ref[...], (8, CH)).T[:, 0:1], (CH, LANES)
    )

    def make_onehot(t, carry):
        entry = o_s[t] * 32 + b_s[t]
        onehot[t] = jnp.where(iota((TARGETS, EDGES), 0) == entry, 1.0, 0.0).astype(BF16)
        return carry

    lax.fori_loop(0, TILES, make_onehot, 0)
    acc[...] = jnp.zeros_like(acc)
    f_send[...] = jnp.zeros_like(f_send)

    for copy in copies:
        copy.wait()

    lane = iota((8, LANES), 1)
    sub = iota((8, LANES), 0)
    group = lane // 32
    pick = jnp.minimum(sub, 3) * 32 + lane % 32
    for px in range(TX + 2):
        for py in range(TY + 2):
            parts = []
            for z in range(3):
                row = jnp.broadcast_to(pos_grid[z, px, py], (8, LANES))
                parts.append(jnp.take_along_axis(row, pick, axis=1))
            pos_cols[px, py] = jnp.where(
                group == 0, parts[0], jnp.where(group == 1, parts[1], parts[2])
            )
            if 1 <= px <= TX and 1 <= py <= TY:
                own_cols[(px - 1) * TY + py - 1] = parts[1]

    def gather(columns, t, x, y, height, m):
        c9 = jnp.broadcast_to(c9_s[t, :, m * LANES : (m + 1) * LANES], (8, LANES))
        loc = jnp.broadcast_to(loc_s[t, :, m * LANES : (m + 1) * LANES], (8, LANES))
        outs = [None] * (height // 8)
        for c in range(9):
            for r in range(height // 8):
                source = columns[x + c // 3, y + c % 3, r * 8 : r * 8 + 8, :]
                got = jnp.take_along_axis(source, loc, axis=1)
                outs[r] = got if c == 0 else jnp.where(c9 == c, got, outs[r])
        return jnp.concatenate(outs, axis=0) if len(outs) > 1 else outs[0]

    def first(t):
        x, y = t // TY, t % TY
        near = jnp.concatenate([gather(pos_cols, t, x, y, 8, m) for m in range(4)], axis=1)
        centre = spread(own_cols[t])
        o = o_s[t]
        ox = (o // 9 - 1).astype(F32) * TILE
        oy = (o // 3 % 3 - 1).astype(F32) * TILE
        oz = (o % 3 - 1).astype(F32) * TILE
        row8 = iota((8, EDGES), 0)
        move = jnp.where(row8 == 0, ox, jnp.where(row8 == 1, oy, jnp.where(row8 == 2, oz, 0.0)))
        vec = jnp.where(row8 < 3, (move + near) - centre, 0.0)
        dist = jnp.sqrt(jnp.sum(vec * vec, axis=0, keepdims=True))
        inv = 1.0 / dist
        u = dist * (1.0 / CUT)
        own_label = centre[3:4]
        near_label = near[3:4]
        live = (own_label >= 0.0) & (near_label >= 0.0) & (u < 1.0)
        u2 = u * u
        u5 = u2 * u2 * u
        env = 1.0 + u5 * u * (-28.0 + u * (48.0 - 21.0 * u))
        denv = (-168.0 / CUT) * u5 * ((1.0 - u) * (1.0 - u))
        weight = jnp.where(live, env, 0.0)
        dweight = jnp.where(live, denv, 0.0)
        orders = (row8 + 1).astype(F32)
        angle = orders * jnp.minimum(u, 1.0)
        turns = jnp.floor(angle + 0.5)
        rest = angle - turns
        parity = turns * 0.5 - jnp.floor(turns * 0.5)
        sign = 1.0 - 4.0 * parity
        rest2 = rest * rest
        sine = sign * rest * polynomial(rest2, SIN)
        cosine = sign * polynomial(rest2, COS)
        radial = sine * inv
        dradial = (orders * (math.pi / CUT) * cosine - radial) * inv
        label = jnp.where(row8 < 2, own_label, near_label)
        hot = jnp.where(label == (row8 % 2).astype(F32), 1.0, 0.0)
        hot = jnp.where(row8 < 4, hot, 0.0)
        table = jnp.concatenate([radial, hot], axis=0)
        h1 = dot(wf_s[...], stack3(table))
        t1 = jnp.tanh(h1)
        s1 = h1 + h1 * t1
        silu1[t] = s1
        slope1[t] = (0.5 + 0.5 * t1) * (1.0 + (h1 - h1 * t1))
        edge = s1 * weight
        env_atom = over_edges(edge) * 0.25
        h2 = dot(w1a_s[...], stack3(edge)) + spread(dot(w1b_s[...], stack3(env_atom)))
        t2 = jnp.tanh(h2)
        s2 = h2 + h2 * t2
        silu2[t] = s2
        slope2[t] = (0.5 + 0.5 * t2) * (1.0 + (h2 - h2 * t2))
        second = edge + weight * s2
        second_s[t] = second
        state = over_edges(weight * second) * 0.25
        qp = dot(w2bc_s[...], stack3(state))
        q_s[t] = qp[:CH]
        lanes16 = iota((16, LANES), 1) // 32
        sent = qp[CH : CH + 16]
        for j in range(1, 4):
            sent = jnp.where(lanes16 == j, qp[CH + 16 * j : CH + 16 * j + 16], sent)
        p_grid[1, 1 + x, 1 + y] = sent
        weight_s[t] = weight
        dweight_s[t] = dweight
        unit_s[t] = vec * inv
        dradial_s[t] = dradial

    def first_step(i, carry):
        for v in range(2):
            first(i * 2 + v)
        return carry

    lax.fori_loop(0, TILES // 2, first_step, 0)

    copies = outward(p_grid, sems, 26)
    for copy in copies:
        copy.start()

    def mix_step(i, carry):
        for v in range(2):
            t = i * 2 + v
            mix_s[t] = dot(w2a_s[...], stack3(second_s[t])) + spread(q_s[t])
        return carry

    lax.fori_loop(0, TILES // 2, mix_step, 0)
    for copy in copies:
        copy.wait()

    def columns_step(i, carry):
        px, py = i // (TY + 2), i % (TY + 2)
        lanes16 = iota((16, LANES), 1) // 32
        parts = [p_grid[z, px, py] for z in range(3)]
        for j in range(4):
            moved = [
                parts[z] if z == j else pltpu.roll(parts[z], ((z - j) * 32) % LANES, 1)
                for z in range(3)
            ]
            p_cols[px, py, 16 * j : 16 * j + 16, :] = jnp.where(
                lanes16 == 0, moved[0], jnp.where(lanes16 == 1, moved[1], moved[2])
            )
        return carry

    lax.fori_loop(0, (TX + 2) * (TY + 2), columns_step, 0)

    def third(t):
        x, y = t // TY, t % TY
        near = jnp.concatenate([gather(p_cols, t, x, y, CH, m) for m in range(4)], axis=1)
        weight = weight_s[t]
        wo = spread(wo_s[...])
        h3 = mix_s[t] + near
        t3 = jnp.tanh(h3)
        s3 = h3 + h3 * t3
        slope3 = (0.5 + 0.5 * t3) * (1.0 + (h3 - h3 * t3))
        ws3 = weight * s3
        out3 = second_s[t] + ws3
        energy = jnp.sum(over_edges(weight * out3) * wo_s[...], axis=0, keepdims=True)
        result_s[t] = energy
        dwacc_s[t] = jnp.sum(wo * (out3 + ws3), axis=0, keepdims=True)
        grad3 = (weight * weight) * wo * slope3
        back_s[t] = grad3
        sum_s[t] = over_edges(grad3)
        high, low = halves(grad3)
        added = dot_t(onehot[t], jnp.concatenate([high, low], axis=0))
        for c in range(9):
            px, py = x + c // 3, y + c % 3
            acc[px, py] = acc[px, py] + added[96 * c : 96 * c + 96]

    def third_step(i, carry):
        third(i)
        return carry

    lax.fori_loop(0, TILES, third_step, 0)

    def fold_step(i, carry):
        px, py = i // (TY + 2), i % (TY + 2)
        lanes16 = iota((16, LANES), 1)
        for z in range(3):
            both = acc[px, py, 32 * z : 32 * z + 32, :]
            both = both + pltpu.roll(both, 64, 1)
            g_send[z, px, py] = jnp.where(lanes16 < 64, both[:16], both[16:])
        return carry

    lax.fori_loop(0, (TX + 2) * (TY + 2), fold_step, 0)
    copies = homeward(g_send, g_recv, sems, 52)
    for copy in copies:
        copy.start()

    def back_step(i, carry):
        for v in range(2):
            t = i * 2 + v
            weight = weight_s[t]
            back_s[t] = weight * spread(wo_s[...]) + dot(w2at_s[...], stack3(back_s[t]))
            q_s[t] = dot(w2bt_s[...], stack3(sum_s[t]))
        return carry

    lax.fori_loop(0, TILES // 2, back_step, 0)
    for copy in copies:
        copy.wait()

    for t in range(TILES):
        x, y = t // TY, t % TY
        total = g_send[1, 1 + x, 1 + y]
        for place in shares(x, y):
            total = total + g_recv[place]
        g_send[1, 1 + x, 1 + y] = total

    def last(t):
        x, y = t // TY, t % TY
        total = g_send[1, 1 + x, 1 + y]
        atoms = jnp.concatenate([total[:, :CH], total[:, CH:]], axis=0)
        atoms = jnp.concatenate([atoms, atoms, atoms, atoms], axis=0)
        returned = lax.dot_general(
            w2ct_s[...],
            atoms,
            (((1,), (1,)), ((), ())),
            preferred_element_type=F32,
            precision=lax.Precision.HIGHEST,
        )
        dstate = spread((q_s[t] + returned) * 0.25)
        weight = weight_s[t]
        s1, s2 = silu1[t], silu2[t]
        dsecond = back_s[t] + weight * dstate
        grad2 = dsecond * (weight * slope2[t])
        denv = dot(w1bt_s[...], stack3(over_edges(grad2))) * 0.25
        dedge = dsecond + dot(w1at_s[...], stack3(grad2)) + spread(denv)
        dweight = dwacc_s[t] + jnp.sum(
            dstate * second_s[t] + dsecond * s2 + dedge * s1, axis=0, keepdims=True
        )
        grad1 = dedge * (weight * slope1[t])
        drad = dot(wrt_s[...], stack3(grad1))[:8]
        ddist = dweight * dweight_s[t] + jnp.sum(
            drad * dradial_s[t], axis=0, keepdims=True
        )
        push = unit_s[t] * ddist
        own = over_edges(push)
        lane1 = iota((1, LANES), 1) // 32
        result_s[t] = jnp.where(
            lane1 == 0,
            own[0:1],
            jnp.where(lane1 == 1, own[1:2], jnp.where(lane1 == 2, own[2:3], result_s[t])),
        )
        o = o_s[t]
        b = b_s[t]
        at_o = iota((32, EDGES), 0) == o
        at_b = jnp.where(iota((LANES, EDGES), 0) % 32 == b, 1.0, 0.0).astype(BF16)
        pieces = []
        for c in range(3):
            pieces.extend(halves(push[c : c + 1]))
        tables = [
            jnp.where(at_o, jnp.broadcast_to(piece.astype(F32), (32, EDGES)), 0.0).astype(BF16)
            for piece in pieces
        ]
        spots = dot_t(jnp.concatenate(tables, axis=0), at_b)
        lane32 = iota((32, LANES), 1) // 32
        comps = [spots[64 * c : 64 * c + 32] + spots[64 * c + 32 : 64 * c + 64] for c in range(3)]
        spots = jnp.where(
            lane32 == 0,
            comps[0],
            jnp.where(lane32 == 1, comps[1], jnp.where(lane32 == 2, comps[2], 0.0)),
        )
        for at in range(27):
            place = (at % 3, x + at // 9, y + at // 3 % 3)
            f_send[place] = f_send[place] + spots[at : at + 1]

    def last_step(i, carry):
        last(i)
        return carry

    lax.fori_loop(0, TILES, last_step, 0)

    copies = homeward(f_send, f_recv, sems, 78)
    for copy in copies:
        copy.start()
    for copy in copies:
        copy.wait()

    found = []
    for t in range(TILES):
        x, y = t // TY, t % TY
        total = f_send[1, 1 + x, 1 + y]
        for place in shares(x, y):
            total = total + f_recv[place]
        found.append(result_s[t] - total)
    rows, cols = iota((LANES, LANES), 0), iota((LANES, LANES), 1)
    place = jnp.where(rows == (cols % 4) * 32 + cols // 4, 1.0, 0.0).astype(F32)
    out_ref[...] = exact_dot(jnp.concatenate(found, axis=0), place)


def local(
    positions, species, counts, neighbours, w_radial, emb_center, emb_nbr, w_first, w_second, w_out
):
    tiles = (TX + 2, TY + 2)
    edges = (TILES, CH, EDGES)
    scratch = [
        pltpu.VMEM((3, *tiles, 1, LANES), F32),
        pltpu.VMEM((TILES, 8, LANES), F32),
        pltpu.VMEM((*tiles, 8, LANES), F32),
        pltpu.VMEM((TILES, 1, EDGES), I32),
        pltpu.VMEM((TILES, 1, EDGES), I32),
        pltpu.VMEM((TILES, 1, EDGES), I32),
        pltpu.VMEM((TILES, 1, EDGES), I32),
        pltpu.VMEM((TILES, TARGETS, EDGES), BF16),
        pltpu.VMEM((CH, 48), BF16),
        pltpu.VMEM((CH, 3 * CH), BF16),
        pltpu.VMEM((CH, 3 * CH), BF16),
        pltpu.VMEM((2 * CH, 3 * CH), BF16),
        pltpu.VMEM((CH, 3 * CH), BF16),
        pltpu.VMEM((CH, 3 * CH), BF16),
        pltpu.VMEM((CH, 3 * CH), BF16),
        pltpu.VMEM((CH, CH), F32),
        pltpu.VMEM((CH, 3 * CH), BF16),
        pltpu.VMEM((CH, 3 * CH), BF16),
        pltpu.VMEM((16, 3 * CH), BF16),
        pltpu.VMEM((CH, LANES), F32),
        pltpu.VMEM(edges, F32),
        pltpu.VMEM(edges, F32),
        pltpu.VMEM(edges, F32),
        pltpu.VMEM(edges, F32),
        pltpu.VMEM(edges, F32),
        pltpu.VMEM(edges, F32),
        pltpu.VMEM(edges, F32),
        pltpu.VMEM((TILES, 1, EDGES), F32),
        pltpu.VMEM((TILES, 1, EDGES), F32),
        pltpu.VMEM((TILES, 1, EDGES), F32),
        pltpu.VMEM((TILES, 8, EDGES), F32),
        pltpu.VMEM((TILES, 8, EDGES), F32),
        pltpu.VMEM((TILES, CH, LANES), F32),
        pltpu.VMEM((TILES, CH, LANES), F32),
        pltpu.VMEM((3, *tiles, 16, LANES), F32),
        pltpu.VMEM((*tiles, CH, LANES), F32),
        pltpu.VMEM((*tiles, 96, LANES), F32),
        pltpu.VMEM((3, *tiles, 16, LANES), F32),
        pltpu.VMEM((3, *tiles, 16, LANES), F32),
        pltpu.VMEM((3, *tiles, 1, LANES), F32),
        pltpu.VMEM((3, *tiles, 1, LANES), F32),
        pltpu.VMEM((TILES, 1, LANES), F32),
        pltpu.SemaphoreType.DMA((104,)),
        pltpu.SemaphoreType.DMA((104,)),
    ]
    vmem = pl.BlockSpec(memory_space=pltpu.VMEM)
    out = pl.pallas_call(
        kernel,
        out_shape=jax.ShapeDtypeStruct((TILES, LANES), F32),
        in_specs=[vmem] * 10,
        out_specs=vmem,
        scratch_shapes=scratch,
        compiler_params=pltpu.CompilerParams(
            collective_id=0, has_side_effects=True, vmem_limit_bytes=58 * 2**20
        ),
        name="forces",
    )(
        positions.reshape(TILES, 3 * SLOTS),
        species.reshape(TILES, SLOTS),
        counts.reshape(TILES, 1),
        neighbours.reshape(TILES, EDGES),
        w_radial,
        emb_center,
        emb_nbr,
        w_first,
        w_second,
        w_out.reshape(1, CH),
    )
    return out.reshape(TX, TY, 1, 4 * SLOTS)


def solution(mesh):
    tiled = P("gx", "gy", "gz", None)
    placed = (tiled, tiled, P("gx", "gy", "gz"), tiled, P(), P(), P(), P(), P(), P())
    return jax.shard_map(local, mesh=mesh, in_specs=placed, out_specs=tiled, check_vma=False)
```

```python
import math

import jax
import jax.numpy as jnp
from jax import lax
from jax.experimental import pallas as pl
from jax.experimental.pallas import tpu as pltpu
from jax.sharding import PartitionSpec as P

F32 = jnp.float32
BF16 = jnp.bfloat16
I32 = jnp.int32

CUT = 5.0
TILE = 8.0
CH = 64
NBR = 16
SLOTS = 32
EDGES = 512
TX = 4
TY = 4
TILES = TX * TY
LANES = 128
TARGETS = 27 * SLOTS

DIRS = [
    (dx, dy, dz)
    for dz in (-1, 1, 0)
    for dx in (-1, 0, 1)
    for dy in (-1, 0, 1)
    if (dx, dy, dz) != (0, 0, 0)
]


def edge_of(step, count):
    if step == 0:
        return pl.ds(1, count)
    return pl.ds(count if step > 0 else 1, 1)


def ghost_of(step, count):
    if step == 0:
        return pl.ds(1, count)
    return pl.ds(count + 1 if step > 0 else 0, 1)


def device_at(step):
    names = ("gx", "gy", "gz")
    place = []
    for name, move in zip(names, step):
        size = lax.axis_size(name)
        place.append(lax.rem(lax.axis_index(name) + (move + size), size))
    return tuple(place)


def outward(buf, sems, base):
    send, recv = sems
    made = []
    for index, (dx, dy, dz) in enumerate(DIRS):
        made.append(
            pltpu.make_async_remote_copy(
                src_ref=buf.at[1, edge_of(dx, TX), edge_of(dy, TY)],
                dst_ref=buf.at[1 - dz, ghost_of(-dx, TX), ghost_of(-dy, TY)],
                send_sem=send.at[base + index],
                recv_sem=recv.at[base + index],
                device_id=device_at((dx, dy, dz)),
                device_id_type=pl.DeviceIdType.MESH,
            )
        )
    return made


def homeward(source, target, sems, base):
    send, recv = sems
    made = []
    for index, (dx, dy, dz) in enumerate(DIRS):
        place = (1 + dz, ghost_of(dx, TX), ghost_of(dy, TY))
        made.append(
            pltpu.make_async_remote_copy(
                src_ref=source.at[place],
                dst_ref=target.at[place],
                send_sem=send.at[base + index],
                recv_sem=recv.at[base + index],
                device_id=device_at((dx, dy, dz)),
                device_id_type=pl.DeviceIdType.MESH,
            )
        )
    return made


FLAT = [(dy, dz) for dy in (0, -1, 1) for dz in (-1, 1, 0) if (dy, dz) != (0, 0)]
FACE = [(dy, dz) for dy in (-1, 0, 1) for dz in (-1, 1, 0)]


def remote(source, target, sems, index, step):
    send, recv = sems
    return pltpu.make_async_remote_copy(
        src_ref=source,
        dst_ref=target,
        send_sem=send.at[index],
        recv_sem=recv.at[index],
        device_id=device_at(step),
        device_id_type=pl.DeviceIdType.MESH,
    )


def outward_row(buf, sems, base, x):
    return [
        remote(
            buf.at[1, 1 + x, edge_of(dy, TY)],
            buf.at[1 - dz, 1 + x, ghost_of(-dy, TY)],
            sems,
            base + index,
            (0, dy, dz),
        )
        for index, (dy, dz) in enumerate(FLAT)
    ]


def outward_face(buf, sems, base, dx):
    x = TX if dx > 0 else 1
    return [
        remote(
            buf.at[1, x, edge_of(dy, TY)],
            buf.at[1 - dz, TX + 1 if dx < 0 else 0, ghost_of(-dy, TY)],
            sems,
            base + index,
            (dx, dy, dz),
        )
        for index, (dy, dz) in enumerate(FACE)
    ]


def homeward_rows(source, target, sems, base, px, count):
    made = []
    for index, (dy, dz) in enumerate(FLAT):
        place = (1 + dz, pl.ds(px, count), ghost_of(dy, TY))
        made.append(remote(source.at[place], target.at[place], sems, base + index, (0, dy, dz)))
    return made


def homeward_face(source, target, sems, base, dx):
    made = []
    for index, (dy, dz) in enumerate(FACE):
        place = (1 + dz, TX + 1 if dx > 0 else 0, ghost_of(dy, TY))
        made.append(remote(source.at[place], target.at[place], sems, base + index, (dx, dy, dz)))
    return made


def shares(x, y):
    found = []
    for dx, dy, dz in DIRS:
        if dx != 0 and x != (0 if dx > 0 else TX - 1):
            continue
        if dy != 0 and y != (0 if dy > 0 else TY - 1):
            continue
        px = x + 1 if dx == 0 else (TX + 1 if dx > 0 else 0)
        py = y + 1 if dy == 0 else (TY + 1 if dy > 0 else 0)
        found.append((1 + dz, px, py))
    return found


def halves(x):
    high = x.astype(BF16)
    low = (x - high.astype(F32)).astype(BF16)
    return high, low


def stack3(x):
    high, low = halves(x)
    return jnp.concatenate([high, low, high], axis=0)


def weight3(w):
    high, low = halves(w)
    return jnp.concatenate([high, high, low], axis=1)


def dot(left, right):
    return lax.dot_general(
        left, right, (((1,), (0,)), ((), ())), preferred_element_type=F32
    )


def dot_t(left, right):
    return lax.dot_general(
        left, right, (((1,), (1,)), ((), ())), preferred_element_type=F32
    )


def exact_dot(left, right):
    return lax.dot_general(
        left,
        right,
        (((1,), (0,)), ((), ())),
        preferred_element_type=F32,
        precision=lax.Precision.HIGHEST,
    )


def over_edges(x):
    total = (x[:, 0:128] + x[:, 128:256]) + (x[:, 256:384] + x[:, 384:512])
    total = total + pltpu.roll(total, 64, 1)
    return total + pltpu.roll(total, 32, 1)


def spread(x):
    return jnp.concatenate([x, x, x, x], axis=1)


def polynomial(x, coefficients):
    total = jnp.full_like(x, coefficients[-1])
    for value in reversed(coefficients[:-1]):
        total = total * x + value
    return total


SIN = [(-1.0) ** i * math.pi ** (2 * i + 1) / math.factorial(2 * i + 1) for i in range(7)]
COS = [(-1.0) ** i * math.pi ** (2 * i) / math.factorial(2 * i) for i in range(8)]


def iota(shape, dim):
    return lax.broadcasted_iota(I32, shape, dim)


def kernel(
    pos_ref, spec_ref, count_ref, nbr_ref, wr_ref, ec_ref, en_ref, w1_ref, w2_ref, wo_ref,
    out_ref,
    pos_grid, own_cols, pos_cols, c9_s, loc_s, o_s, b_s,
    onehot, wf_s, w1a_s, w1b_s, w2bc_s, w2a_s, w2at_s, w2bt_s, w2ct_s, w1bt_s, wo_s,
    silu2, wslope2, second_s, slide1, slide2, slide_s, mix_s, silu3, grad3_s,
    weight_s, dweight_s, unit_s, q_s, m2_s, sum2_s, direct_s, return_s,
    p_grid, p_cols, acc, g_send, g_recv, f_tile, f_send, f_recv, result_s,
    send_sem, recv_sem,
):
    sems = (send_sem, recv_sem)
    barrier = pltpu.get_barrier_semaphore()
    for step in DIRS:
        pl.semaphore_signal(
            barrier, inc=1, device_id=device_at(step), device_id_type=pl.DeviceIdType.MESH
        )

    rows, cols = iota((96, LANES), 0), iota((96, LANES), 1)
    place = jnp.where(cols < 96, jnp.where(rows == (cols % 32) * 3 + cols // 32, 1.0, 0.0), 0.0)
    counts = []
    for x in range(TX):
        wide = jnp.broadcast_to(count_ref[x], (TY, TY))
        diagonal = jnp.where(iota((TY, TY), 0) == iota((TY, TY), 1), wide, 0)
        counts.append(jnp.sum(diagonal.astype(F32), axis=1, keepdims=True))
    count = jnp.concatenate(counts, axis=0).astype(I32)
    labels = jnp.where(iota((TILES, SLOTS), 1) < count, spec_ref[...], -1).astype(F32)
    shift = jnp.where(iota((SLOTS, LANES), 1) == iota((SLOTS, LANES), 0) + 96, 1.0, 0.0).astype(F32)
    packed = exact_dot(pos_ref[...], place) + exact_dot(labels, shift)
    for t in range(TILES):
        pos_grid[1, 1 + t // TY, 1 + t % TY] = packed[t : t + 1]

    half = 0.5
    table = jnp.concatenate([wr_ref[...], ec_ref[...], en_ref[...], jnp.zeros((4, CH), F32)], axis=0)
    wf_s[...] = weight3(table.T * half)
    w1 = w1_ref[...]
    w2 = w2_ref[...]
    w1a, w1b = w1[:, :CH], w1[:, CH:]
    w2a, w2b, w2c = w2[:, :CH], w2[:, CH : 2 * CH], w2[:, 2 * CH :]
    w1a_s[...] = weight3(w1a * half)
    w1b_s[...] = weight3(w1b * half)
    w2bc_s[...] = weight3(jnp.concatenate([w2b, w2c], axis=0) * half)
    w2a_s[...] = weight3(w2a * half)
    w2at_s[...] = weight3(w2a.T)
    w2bt_s[...] = weight3(w2b.T)
    w2ct_s[...] = w2c.T
    w1bt_s[...] = weight3(w1b.T)
    wo_s[...] = jnp.broadcast_to(
        jnp.broadcast_to(wo_ref[...], (8, CH)).T[:, 0:1], (CH, LANES)
    )

    entry = jnp.concatenate([nbr_ref[pl.ds(q, TILES, stride=4), :] for q in range(4)], axis=1)
    order = jnp.where(
        iota((EDGES, EDGES), 0) == (iota((EDGES, EDGES), 1) % 32) * 16 + iota((EDGES, EDGES), 1) // 32,
        1.0,
        0.0,
    ).astype(BF16)
    o_new = dot((entry // 32).astype(F32).astype(BF16), order).astype(I32)
    b_new = dot((entry % 32).astype(F32).astype(BF16), order).astype(I32)
    c9_new = o_new // 3
    loc_new = (o_new % 3) * 32 + b_new
    for t in range(TILES):
        o_s[t] = o_new[t : t + 1]
        b_s[t] = b_new[t : t + 1]
        c9_s[t] = c9_new[t : t + 1]
        loc_s[t] = loc_new[t : t + 1]

    pl.semaphore_wait(barrier, len(DIRS))
    copies = outward(pos_grid, sems, 0)
    for copy in copies:
        copy.start()

    def make_onehot(t, carry):
        entry = o_s[t] * 32 + b_s[t]
        onehot[t] = jnp.where(iota((TARGETS, EDGES), 0) == entry, 1.0, 0.0).astype(BF16)
        return carry

    lax.fori_loop(0, TILES, make_onehot, 0)
    acc[...] = jnp.zeros_like(acc)

    for copy in copies:
        copy.wait()

    lane = iota((8, LANES), 1)
    sub = iota((8, LANES), 0)
    group = lane // 32
    pick = jnp.minimum(sub, 3) * 32 + lane % 32
    for px in range(TX + 2):
        for py in range(TY + 2):
            parts = []
            for z in range(3):
                row = jnp.broadcast_to(pos_grid[z, px, py], (8, LANES))
                parts.append(jnp.take_along_axis(row, pick, axis=1))
            pos_cols[px, py] = jnp.where(
                group == 0, parts[0], jnp.where(group == 1, parts[1], parts[2])
            )
            if 1 <= px <= TX and 1 <= py <= TY:
                own_cols[(px - 1) * TY + py - 1] = parts[1]

    def gather(columns, t, x, y, height, m):
        c9 = jnp.broadcast_to(c9_s[t, :, m * LANES : (m + 1) * LANES], (8, LANES))
        loc = jnp.broadcast_to(loc_s[t, :, m * LANES : (m + 1) * LANES], (8, LANES))
        outs = [None] * (height // 8)
        for c in range(9):
            for r in range(height // 8):
                source = columns[x + c // 3, y + c % 3, r * 8 : r * 8 + 8, :]
                got = jnp.take_along_axis(source, loc, axis=1)
                outs[r] = got if c == 0 else jnp.where(c9 == c, got, outs[r])
        return jnp.concatenate(outs, axis=0) if len(outs) > 1 else outs[0]

    def first(x, y):
        t = x * TY + y
        near = jnp.concatenate([gather(pos_cols, t, x, y, 8, m) for m in range(4)], axis=1)
        centre = spread(own_cols[t])
        o = o_s[t]
        ox = (o // 9 - 1).astype(F32) * TILE
        oy = (o // 3 % 3 - 1).astype(F32) * TILE
        oz = (o % 3 - 1).astype(F32) * TILE
        row8 = iota((8, EDGES), 0)
        move = jnp.where(row8 == 0, ox, jnp.where(row8 == 1, oy, jnp.where(row8 == 2, oz, 0.0)))
        vec = jnp.where(row8 < 3, (move + near) - centre, 0.0)
        dist = jnp.sqrt(jnp.sum(vec * vec, axis=0, keepdims=True))
        inv = 1.0 / dist
        u = dist * (1.0 / CUT)
        own_label = centre[3:4]
        near_label = near[3:4]
        live = (own_label >= 0.0) & (near_label >= 0.0) & (u < 1.0)
        u2 = u * u
        u5 = u2 * u2 * u
        env = 1.0 + u5 * u * (-28.0 + u * (48.0 - 21.0 * u))
        denv = (-168.0 / CUT) * u5 * ((1.0 - u) * (1.0 - u))
        weight = jnp.where(live, env, 0.0)
        dweight = jnp.where(live, denv, 0.0)
        orders = (row8 + 1).astype(F32)
        angle = orders * jnp.minimum(u, 1.0)
        turns = jnp.floor(angle + 0.5)
        rest = angle - turns
        parity = turns * 0.5 - jnp.floor(turns * 0.5)
        sign = 1.0 - 4.0 * parity
        rest2 = rest * rest
        sine = sign * rest * polynomial(rest2, SIN)
        cosine = sign * polynomial(rest2, COS)
        radial = sine * inv
        dradial = (orders * (math.pi / CUT) * cosine - radial) * inv
        label = jnp.where(row8 < 2, own_label, near_label)
        hot = jnp.where(label == (row8 % 2).astype(F32), 1.0, 0.0)
        hot = jnp.where(row8 < 4, hot, 0.0)
        h1 = dot(wf_s[...], stack3(jnp.concatenate([radial, hot], axis=0)))
        slide = dot(wf_s[...], stack3(jnp.concatenate([dradial, jnp.zeros_like(hot)], axis=0)))
        t1 = jnp.tanh(h1)
        s1 = h1 + h1 * t1
        slope1 = (1.0 + t1) * (1.0 + (h1 - h1 * t1))
        edge = s1 * weight
        slide1[t] = dweight * s1 + weight * (slope1 * slide)
        env_atom = over_edges(edge) * 0.25
        h2 = dot(w1a_s[...], stack3(edge)) + spread(dot(w1b_s[...], stack3(env_atom)))
        t2 = jnp.tanh(h2)
        s2 = h2 + h2 * t2
        silu2[t] = s2
        wslope2[t] = weight * ((0.5 + 0.5 * t2) * (1.0 + (h2 - h2 * t2)))
        second = edge + weight * s2
        second_s[t] = second
        state = over_edges(weight * second) * 0.25
        qp = dot(w2bc_s[...], stack3(state))
        q_s[t] = qp[:CH]
        lanes16 = iota((16, LANES), 1) // 32
        sent = qp[CH : CH + 16]
        for j in range(1, 4):
            sent = jnp.where(lanes16 == j, qp[CH + 16 * j : CH + 16 * j + 16], sent)
        p_grid[1, 1 + x, 1 + y] = sent
        weight_s[t] = weight
        dweight_s[t] = dweight
        unit_s[t] = vec * inv

    def row_of(i):
        return (3 * i) % 4

    def first_step(i, carry):
        x = row_of(i)
        for y in range(TY):
            first(x, y)
        for copy in outward_row(p_grid, sems, 26 + 8 * i, x):
            copy.start()

        @pl.when(i == 0)
        def _():
            for copy in outward_face(p_grid, sems, 58, -1):
                copy.start()

        @pl.when(i == 1)
        def _():
            for copy in outward_face(p_grid, sems, 67, 1):
                copy.start()

        return carry

    lax.fori_loop(0, TX, first_step, 0)

    def mix_step(i, carry):
        for v in range(4):
            t = i * 4 + v
            weight, dweight = weight_s[t], dweight_s[t]
            mix_s[t] = dot(w2a_s[...], stack3(second_s[t])) + spread(q_s[t])
            first_slide = slide1[t]
            wslope = wslope2[t]
            moved = dot(w1a_s[...], stack3(first_slide))
            full = first_slide + dweight * silu2[t] + (2.0 * wslope) * moved
            slide2[t] = full
            slide_s[t] = weight * full + dweight * second_s[t]
            m2_s[t] = over_edges(weight * wslope)
        return carry

    lax.fori_loop(0, TILES // 4, mix_step, 0)
    for i in range(TX):
        for copy in outward_row(p_grid, sems, 26 + 8 * i, row_of(i)):
            copy.wait()
    for copy in outward_face(p_grid, sems, 58, -1):
        copy.wait()
    for copy in outward_face(p_grid, sems, 67, 1):
        copy.wait()

    def columns_step(px, carry):
        lanes16 = iota((16, LANES), 1) // 32
        for py in range(TY + 2):
            parts = [p_grid[z, px, py] for z in range(3)]
            for j in range(4):
                moved = [
                    parts[z] if z == j else pltpu.roll(parts[z], ((z - j) * 32) % LANES, 1)
                    for z in range(3)
                ]
                p_cols[px, py, 16 * j : 16 * j + 16, :] = jnp.where(
                    lanes16 == 0, moved[0], jnp.where(lanes16 == 1, moved[1], moved[2])
                )
        return carry

    lax.fori_loop(0, TX + 2, columns_step, 0)

    def third(x, y):
        t = x * TY + y
        near = jnp.concatenate([gather(p_cols, t, x, y, CH, m) for m in range(4)], axis=1)
        weight = weight_s[t]
        h3 = mix_s[t] + near
        t3 = jnp.tanh(h3)
        silu3[t] = h3 + h3 * t3
        slope3 = (0.5 + 0.5 * t3) * (1.0 + (h3 - h3 * t3))
        grad3 = (weight * weight) * spread(wo_s[...]) * slope3
        grad3_s[t] = grad3
        high, low = halves(grad3)
        added = dot_t(onehot[t], jnp.concatenate([high, low], axis=0))
        for c in range(9):
            px, py = x + c // 3, y + c % 3
            acc[px, py] = acc[px, py] + added[96 * c : 96 * c + 96]

    def fold(px):
        lanes16 = iota((16, LANES), 1)
        for py in range(TY + 2):
            for z in range(3):
                both = acc[px, py, 32 * z : 32 * z + 32, :]
                both = both + pltpu.roll(both, 64, 1)
                g_send[z, px, py] = jnp.where(lanes16 < 64, both[:16], both[16:])

    def third_step(i, carry):
        x = row_of(i)
        for y in range(TY):
            third(x, y)

        @pl.when(i == 0)
        def _():
            fold(0)
            for copy in homeward_face(g_send, g_recv, sems, 76, -1):
                copy.start()

        @pl.when(i == 1)
        def _():
            fold(TX + 1)
            for copy in homeward_face(g_send, g_recv, sems, 85, 1):
                copy.start()

        @pl.when(i == 2)
        def _():
            fold(TX)
            for copy in homeward_rows(g_send, g_recv, sems, 94, TX, 1):
                copy.start()

        return carry

    lax.fori_loop(0, TX, third_step, 0)
    for px in range(1, TX):
        fold(px)
    for copy in homeward_rows(g_send, g_recv, sems, 102, 1, TX - 1):
        copy.start()

    def back_step(i, carry):
        for v in range(4):
            t = i * 4 + v
            weight, dweight = weight_s[t], dweight_s[t]
            wo = spread(wo_s[...])
            ws3 = weight * silu3[t]
            out3 = second_s[t] + ws3
            energy = jnp.sum(over_edges(weight * out3) * wo_s[...], axis=0, keepdims=True)
            result_s[t] = energy
            grad3 = grad3_s[t]
            back = weight * wo + dot(w2at_s[...], stack3(grad3))
            direct_s[t] = jnp.sum(
                back * slide2[t] + (dweight * wo) * (out3 + ws3), axis=0, keepdims=True
            )
            sum2_s[t] = over_edges(back * wslope2[t])
            q_s[t] = dot(w2bt_s[...], stack3(over_edges(grad3)))
        return carry

    lax.fori_loop(0, TILES // 4, back_step, 0)
    for copy in homeward_face(g_send, g_recv, sems, 76, -1):
        copy.wait()
    for copy in homeward_face(g_send, g_recv, sems, 85, 1):
        copy.wait()
    for copy in homeward_rows(g_send, g_recv, sems, 94, TX, 1):
        copy.wait()
    for copy in homeward_rows(g_send, g_recv, sems, 102, 1, TX - 1):
        copy.wait()

    for t in range(TILES):
        x, y = t // TY, t % TY
        total = g_send[1, 1 + x, 1 + y]
        for place in shares(x, y):
            total = total + g_recv[place]
        return_s[t] = total

    def last(t):
        total = return_s[t]
        atoms = jnp.concatenate([total[:, :CH], total[:, CH:]], axis=0)
        atoms = jnp.concatenate([atoms, atoms, atoms, atoms], axis=0)
        returned = lax.dot_general(
            w2ct_s[...],
            atoms,
            (((1,), (1,)), ((), ())),
            preferred_element_type=F32,
            precision=lax.Precision.HIGHEST,
        )
        dstate = (q_s[t] + returned) * 0.25
        denv = dot(w1bt_s[...], stack3(sum2_s[t] + dstate * m2_s[t])) * 0.25
        ddist = direct_s[t] + jnp.sum(
            spread(dstate) * slide_s[t] + spread(denv) * slide1[t], axis=0, keepdims=True
        )
        push = unit_s[t] * ddist
        own = over_edges(push)
        lane1 = iota((1, LANES), 1) // 32
        result_s[t] = jnp.where(
            lane1 == 0,
            own[0:1],
            jnp.where(lane1 == 1, own[1:2], jnp.where(lane1 == 2, own[2:3], result_s[t])),
        )
        o = o_s[t]
        b = b_s[t]
        at_o = iota((32, EDGES), 0) == o
        at_b = jnp.where(iota((LANES, EDGES), 0) % 32 == b, 1.0, 0.0).astype(BF16)
        pieces = []
        for c in range(3):
            pieces.extend(halves(push[c : c + 1]))
        tables = [
            jnp.where(at_o, jnp.broadcast_to(piece.astype(F32), (32, EDGES)), 0.0).astype(BF16)
            for piece in pieces
        ]
        spots = dot_t(jnp.concatenate(tables, axis=0), at_b)
        lane32 = iota((32, LANES), 1) // 32
        comps = [spots[64 * c : 64 * c + 32] + spots[64 * c + 32 : 64 * c + 64] for c in range(3)]
        f_tile[t] = jnp.where(
            lane32 == 0,
            comps[0],
            jnp.where(lane32 == 1, comps[1], jnp.where(lane32 == 2, comps[2], 0.0)),
        )

    def last_step(i, carry):
        for v in range(4):
            last(i * 4 + v)
        return carry

    lax.fori_loop(0, TILES // 4, last_step, 0)

    for px in range(TX + 2):
        for py in range(TY + 2):
            for z in range(3):
                total = None
                for c in range(9):
                    x, y = px - c // 3, py - c % 3
                    if 0 <= x < TX and 0 <= y < TY:
                        at = 3 * c + z
                        part = f_tile[x * TY + y, at : at + 1, :]
                        total = part if total is None else total + part
                f_send[z, px, py] = total

    copies = homeward(f_send, f_recv, sems, 110)
    for copy in copies:
        copy.start()
    for copy in copies:
        copy.wait()

    found = []
    for t in range(TILES):
        x, y = t // TY, t % TY
        total = f_send[1, 1 + x, 1 + y]
        for place in shares(x, y):
            total = total + f_recv[place]
        found.append(result_s[t] - total)
    rows, cols = iota((LANES, LANES), 0), iota((LANES, LANES), 1)
    place = jnp.where(rows == (cols % 4) * 32 + cols // 4, 1.0, 0.0).astype(F32)
    out_ref[...] = exact_dot(jnp.concatenate(found, axis=0), place)


def local(
    positions, species, counts, neighbours, w_radial, emb_center, emb_nbr, w_first, w_second, w_out
):
    tiles = (TX + 2, TY + 2)
    edges = pltpu.VMEM((TILES, CH, EDGES), F32)
    row = pltpu.VMEM((TILES, 1, EDGES), F32)
    entries = pltpu.VMEM((TILES, 1, EDGES), I32)
    atoms = pltpu.VMEM((TILES, CH, LANES), F32)
    wide = pltpu.VMEM((CH, 3 * CH), BF16)
    small_grid = pltpu.VMEM((3, *tiles, 1, LANES), F32)
    grid = pltpu.VMEM((3, *tiles, 16, LANES), F32)
    scratch = dict(
        pos_grid=small_grid,
        own_cols=pltpu.VMEM((TILES, 8, LANES), F32),
        pos_cols=pltpu.VMEM((*tiles, 8, LANES), F32),
        c9_s=entries,
        loc_s=entries,
        o_s=entries,
        b_s=entries,
        onehot=pltpu.VMEM((TILES, TARGETS, EDGES), BF16),
        wf_s=pltpu.VMEM((CH, 48), BF16),
        w1a_s=wide,
        w1b_s=wide,
        w2bc_s=pltpu.VMEM((2 * CH, 3 * CH), BF16),
        w2a_s=wide,
        w2at_s=wide,
        w2bt_s=wide,
        w2ct_s=pltpu.VMEM((CH, CH), F32),
        w1bt_s=wide,
        wo_s=pltpu.VMEM((CH, LANES), F32),
        silu2=edges,
        wslope2=edges,
        second_s=edges,
        slide1=edges,
        slide2=edges,
        slide_s=edges,
        mix_s=edges,
        silu3=edges,
        grad3_s=edges,
        weight_s=row,
        dweight_s=row,
        unit_s=pltpu.VMEM((TILES, 8, EDGES), F32),
        q_s=atoms,
        m2_s=atoms,
        sum2_s=atoms,
        direct_s=row,
        return_s=pltpu.VMEM((TILES, 16, LANES), F32),
        p_grid=grid,
        p_cols=pltpu.VMEM((*tiles, CH, LANES), F32),
        acc=pltpu.VMEM((*tiles, 96, LANES), F32),
        g_send=grid,
        g_recv=grid,
        f_tile=pltpu.VMEM((TILES, 32, LANES), F32),
        f_send=small_grid,
        f_recv=small_grid,
        result_s=pltpu.VMEM((TILES, 1, LANES), F32),
        send_sem=pltpu.SemaphoreType.DMA((136,)),
        recv_sem=pltpu.SemaphoreType.DMA((136,)),
    )
    vmem = pl.BlockSpec(memory_space=pltpu.VMEM)
    out = pl.pallas_call(
        kernel,
        out_shape=jax.ShapeDtypeStruct((TILES, LANES), F32),
        in_specs=[vmem] * 10,
        out_specs=vmem,
        scratch_shapes=scratch,
        compiler_params=pltpu.CompilerParams(
            collective_id=0, has_side_effects=True, vmem_limit_bytes=60 * 2**20
        ),
        name="forces",
    )(
        positions.reshape(TILES, 3 * SLOTS),
        species.reshape(TILES, SLOTS),
        counts.transpose(0, 2, 1),
        neighbours.reshape(4 * TILES, LANES),
        w_radial.T,
        emb_center.T,
        emb_nbr.T,
        w_first,
        w_second,
        w_out.reshape(1, CH),
    )
    return out.reshape(TX, TY, 1, 4 * SLOTS)


def solution(mesh):
    tiled = P("gx", "gy", "gz", None)
    placed = (tiled, tiled, P("gx", "gy", "gz"), tiled, P(), P(), P(), P(), P(), P())
    return jax.shard_map(local, mesh=mesh, in_specs=placed, out_specs=tiled, check_vma=False)
```

```python
import math

import jax
import jax.numpy as jnp
from jax import lax
from jax.experimental import pallas as pl
from jax.experimental.pallas import tpu as pltpu
from jax.sharding import PartitionSpec as P

F32 = jnp.float32
BF16 = jnp.bfloat16
I32 = jnp.int32

CUT = 5.0
TILE = 8.0
CH = 64
NBR = 16
SLOTS = 32
EDGES = 512
TX = 4
TY = 4
TILES = TX * TY
LANES = 128
TARGETS = 27 * SLOTS

DIRS = [
    (dx, dy, dz)
    for dz in (-1, 1, 0)
    for dx in (-1, 0, 1)
    for dy in (-1, 0, 1)
    if (dx, dy, dz) != (0, 0, 0)
]


def edge_of(step, count):
    if step == 0:
        return pl.ds(1, count)
    return pl.ds(count if step > 0 else 1, 1)


def ghost_of(step, count):
    if step == 0:
        return pl.ds(1, count)
    return pl.ds(count + 1 if step > 0 else 0, 1)


def device_at(step):
    names = ("gx", "gy", "gz")
    place = []
    for name, move in zip(names, step):
        size = lax.axis_size(name)
        place.append(lax.rem(lax.axis_index(name) + (move + size), size))
    return tuple(place)


def outward(buf, sems, base):
    send, recv = sems
    made = []
    for index, (dx, dy, dz) in enumerate(DIRS):
        made.append(
            pltpu.make_async_remote_copy(
                src_ref=buf.at[1, edge_of(dx, TX), edge_of(dy, TY)],
                dst_ref=buf.at[1 - dz, ghost_of(-dx, TX), ghost_of(-dy, TY)],
                send_sem=send.at[base + index],
                recv_sem=recv.at[base + index],
                device_id=device_at((dx, dy, dz)),
                device_id_type=pl.DeviceIdType.MESH,
            )
        )
    return made


def homeward(source, target, sems, base):
    send, recv = sems
    made = []
    for index, (dx, dy, dz) in enumerate(DIRS):
        place = (1 + dz, ghost_of(dx, TX), ghost_of(dy, TY))
        made.append(
            pltpu.make_async_remote_copy(
                src_ref=source.at[place],
                dst_ref=target.at[place],
                send_sem=send.at[base + index],
                recv_sem=recv.at[base + index],
                device_id=device_at((dx, dy, dz)),
                device_id_type=pl.DeviceIdType.MESH,
            )
        )
    return made


FLAT = [(dy, dz) for dy in (0, -1, 1) for dz in (-1, 1, 0) if (dy, dz) != (0, 0)]
FACE = [(dy, dz) for dy in (-1, 0, 1) for dz in (-1, 1, 0)]


def remote(source, target, sems, index, step):
    send, recv = sems
    return pltpu.make_async_remote_copy(
        src_ref=source,
        dst_ref=target,
        send_sem=send.at[index],
        recv_sem=recv.at[index],
        device_id=device_at(step),
        device_id_type=pl.DeviceIdType.MESH,
    )


def outward_row(buf, sems, base, x):
    return [
        remote(
            buf.at[1, 1 + x, edge_of(dy, TY)],
            buf.at[1 - dz, 1 + x, ghost_of(-dy, TY)],
            sems,
            base + index,
            (0, dy, dz),
        )
        for index, (dy, dz) in enumerate(FLAT)
    ]


def outward_face(buf, sems, base, dx):
    x = TX if dx > 0 else 1
    return [
        remote(
            buf.at[1, x, edge_of(dy, TY)],
            buf.at[1 - dz, TX + 1 if dx < 0 else 0, ghost_of(-dy, TY)],
            sems,
            base + index,
            (dx, dy, dz),
        )
        for index, (dy, dz) in enumerate(FACE)
    ]


def homeward_rows(source, target, sems, base, px, count):
    made = []
    for index, (dy, dz) in enumerate(FLAT):
        place = (1 + dz, pl.ds(px, count), ghost_of(dy, TY))
        made.append(remote(source.at[place], target.at[place], sems, base + index, (0, dy, dz)))
    return made


def homeward_face(source, target, sems, base, dx):
    made = []
    for index, (dy, dz) in enumerate(FACE):
        place = (1 + dz, TX + 1 if dx > 0 else 0, ghost_of(dy, TY))
        made.append(remote(source.at[place], target.at[place], sems, base + index, (dx, dy, dz)))
    return made


def shares(x, y):
    found = []
    for dx, dy, dz in DIRS:
        if dx != 0 and x != (0 if dx > 0 else TX - 1):
            continue
        if dy != 0 and y != (0 if dy > 0 else TY - 1):
            continue
        px = x + 1 if dx == 0 else (TX + 1 if dx > 0 else 0)
        py = y + 1 if dy == 0 else (TY + 1 if dy > 0 else 0)
        found.append((1 + dz, px, py))
    return found


def halves(x):
    high = x.astype(BF16)
    low = (x - high.astype(F32)).astype(BF16)
    return high, low


def stack3(x):
    high, low = halves(x)
    return jnp.concatenate([high, low, high], axis=0)


def weight3(w):
    high, low = halves(w)
    return jnp.concatenate([high, high, low], axis=1)


def dot(left, right):
    return lax.dot_general(
        left, right, (((1,), (0,)), ((), ())), preferred_element_type=F32
    )


def dot_t(left, right):
    return lax.dot_general(
        left, right, (((1,), (1,)), ((), ())), preferred_element_type=F32
    )


def exact_dot(left, right):
    return lax.dot_general(
        left,
        right,
        (((1,), (0,)), ((), ())),
        preferred_element_type=F32,
        precision=lax.Precision.HIGHEST,
    )


def over_edges(x):
    total = (x[:, 0:128] + x[:, 128:256]) + (x[:, 256:384] + x[:, 384:512])
    total = total + pltpu.roll(total, 64, 1)
    return total + pltpu.roll(total, 32, 1)


def spread(x):
    return jnp.concatenate([x, x, x, x], axis=1)


def lane_group(shape):
    return iota(shape, 1) // 32


def in_row(tiles):
    group = lane_group(tiles[0].shape)
    total = tiles[0]
    for y in range(1, TY):
        total = jnp.where(group == y, tiles[y], total)
    return total


def of_tile(row, y):
    place = y * 32 + iota((8, LANES), 1) % 32
    parts = [
        jnp.take_along_axis(row[r : r + 8], place, axis=1) for r in range(0, row.shape[0], 8)
    ]
    return jnp.concatenate(parts, axis=0)


def polynomial(x, coefficients):
    total = jnp.full_like(x, coefficients[-1])
    for value in reversed(coefficients[:-1]):
        total = total * x + value
    return total


SIN = [(-1.0) ** i * math.pi ** (2 * i + 1) / math.factorial(2 * i + 1) for i in range(7)]
COS = [(-1.0) ** i * math.pi ** (2 * i) / math.factorial(2 * i) for i in range(8)]


def iota(shape, dim):
    return lax.broadcasted_iota(I32, shape, dim)


def kernel(
    pos_ref, spec_ref, count_ref, nbr_ref, wr_ref, ec_ref, en_ref, w1_ref, w2_ref, wo_ref,
    out_ref,
    pos_grid, own_cols, pos_cols, c9_s, loc_s, o_s, b_s,
    onehot, wf_s, w1a_s, w1b_s, w2bc_s, w2a_s, w2at_s, w2bt_s, w2ct_s, w1bt_s, wo_s,
    silu2, wslope2, second_s, slide1, slide2, slide_s, mix_s, silu3, grad3_s,
    weight_s, dweight_s, unit_s, q_s, m2_s, sum2_s, direct_s, return_s,
    p_grid, p_cols, acc, g_send, g_recv, f_tile, f_send, f_recv, result_s,
    send_sem, recv_sem,
):
    sems = (send_sem, recv_sem)
    barrier = pltpu.get_barrier_semaphore()
    for step in DIRS:
        pl.semaphore_signal(
            barrier, inc=1, device_id=device_at(step), device_id_type=pl.DeviceIdType.MESH
        )

    rows, cols = iota((96, LANES), 0), iota((96, LANES), 1)
    place = jnp.where(cols < 96, jnp.where(rows == (cols % 32) * 3 + cols // 32, 1.0, 0.0), 0.0)
    counts = []
    for x in range(TX):
        wide = jnp.broadcast_to(count_ref[x], (TY, TY))
        diagonal = jnp.where(iota((TY, TY), 0) == iota((TY, TY), 1), wide, 0)
        counts.append(jnp.sum(diagonal.astype(F32), axis=1, keepdims=True))
    count = jnp.concatenate(counts, axis=0).astype(I32)
    labels = jnp.where(iota((TILES, SLOTS), 1) < count, spec_ref[...], -1).astype(F32)
    shift = jnp.where(iota((SLOTS, LANES), 1) == iota((SLOTS, LANES), 0) + 96, 1.0, 0.0).astype(F32)
    packed = exact_dot(pos_ref[...], place) + exact_dot(labels, shift)
    for t in range(TILES):
        pos_grid[1, 1 + t // TY, 1 + t % TY] = packed[t : t + 1]

    pl.semaphore_wait(barrier, len(DIRS))
    copies = outward(pos_grid, sems, 0)
    for copy in copies:
        copy.start()

    half = 0.5
    table = jnp.concatenate([wr_ref[...], ec_ref[...], en_ref[...], jnp.zeros((4, CH), F32)], axis=0)
    wf_s[...] = weight3(table.T * half)
    w1 = w1_ref[...]
    w2 = w2_ref[...]
    w1a, w1b = w1[:, :CH], w1[:, CH:]
    w2a, w2b, w2c = w2[:, :CH], w2[:, CH : 2 * CH], w2[:, 2 * CH :]
    w1a_s[...] = weight3(w1a * half)
    w1b_s[...] = weight3(w1b * half)
    w2bc_s[...] = weight3(jnp.concatenate([w2b, w2c], axis=0) * half)
    w2a_s[...] = weight3(w2a * half)
    w2at_s[...] = weight3(w2a.T)
    w2bt_s[...] = weight3(w2b.T)
    w2ct_s[...] = jnp.concatenate(halves(w2c.T), axis=0)
    w1bt_s[...] = weight3(w1b.T)
    wo_s[...] = jnp.broadcast_to(
        jnp.broadcast_to(wo_ref[...], (8, CH)).T[:, 0:1], (CH, LANES)
    )

    entry = jnp.concatenate([nbr_ref[pl.ds(q, TILES, stride=4), :] for q in range(4)], axis=1)
    order = jnp.where(
        iota((EDGES, EDGES), 0) == (iota((EDGES, EDGES), 1) % 32) * 16 + iota((EDGES, EDGES), 1) // 32,
        1.0,
        0.0,
    ).astype(BF16)
    o_new = dot((entry // 32).astype(F32).astype(BF16), order).astype(I32)
    b_new = dot((entry % 32).astype(F32).astype(BF16), order).astype(I32)
    c9_new = o_new // 3
    loc_new = (o_new % 3) * 32 + b_new
    for t in range(TILES):
        o_s[t] = o_new[t : t + 1]
        b_s[t] = b_new[t : t + 1]
        c9_s[t] = c9_new[t : t + 1]
        loc_s[t] = loc_new[t : t + 1]

    def make_onehot(t, carry):
        entry = o_s[t] * 32 + b_s[t]
        onehot[t] = jnp.where(iota((TARGETS, EDGES), 0) == entry, 1.0, 0.0).astype(BF16)
        return carry

    lax.fori_loop(0, TILES, make_onehot, 0)
    acc[...] = jnp.zeros_like(acc)

    for copy in copies:
        copy.wait()

    lane = iota((8, LANES), 1)
    sub = iota((8, LANES), 0)
    group = lane // 32
    pick = jnp.minimum(sub, 3) * 32 + lane % 32
    for px in range(TX + 2):
        for py in range(TY + 2):
            parts = []
            for z in range(3):
                row = jnp.broadcast_to(pos_grid[z, px, py], (8, LANES))
                parts.append(jnp.take_along_axis(row, pick, axis=1))
            pos_cols[px, py] = jnp.where(
                group == 0, parts[0], jnp.where(group == 1, parts[1], parts[2])
            )
            if 1 <= px <= TX and 1 <= py <= TY:
                own_cols[(px - 1) * TY + py - 1] = parts[1]

    def gather(columns, t, x, y, height, m):
        c9 = jnp.broadcast_to(c9_s[t, :, m * LANES : (m + 1) * LANES], (8, LANES))
        loc = jnp.broadcast_to(loc_s[t, :, m * LANES : (m + 1) * LANES], (8, LANES))
        outs = [None] * (height // 8)
        for c in range(9):
            for r in range(height // 8):
                source = columns[x + c // 3, y + c % 3, r * 8 : r * 8 + 8, :]
                got = jnp.take_along_axis(source, loc, axis=1)
                outs[r] = got if c == 0 else jnp.where(c9 == c, got, outs[r])
        return jnp.concatenate(outs, axis=0) if len(outs) > 1 else outs[0]

    def first(x, y):
        t = x * TY + y
        near = jnp.concatenate([gather(pos_cols, t, x, y, 8, m) for m in range(4)], axis=1)
        centre = spread(own_cols[t])
        o = o_s[t]
        ox = (o // 9 - 1).astype(F32) * TILE
        oy = (o // 3 % 3 - 1).astype(F32) * TILE
        oz = (o % 3 - 1).astype(F32) * TILE
        row8 = iota((8, EDGES), 0)
        move = jnp.where(row8 == 0, ox, jnp.where(row8 == 1, oy, jnp.where(row8 == 2, oz, 0.0)))
        vec = jnp.where(row8 < 3, (move + near) - centre, 0.0)
        dist = jnp.sqrt(jnp.sum(vec * vec, axis=0, keepdims=True))
        inv = 1.0 / dist
        u = dist * (1.0 / CUT)
        own_label = centre[3:4]
        near_label = near[3:4]
        live = (own_label >= 0.0) & (near_label >= 0.0) & (u < 1.0)
        u2 = u * u
        u5 = u2 * u2 * u
        env = 1.0 + u5 * u * (-28.0 + u * (48.0 - 21.0 * u))
        denv = (-168.0 / CUT) * u5 * ((1.0 - u) * (1.0 - u))
        weight = jnp.where(live, env, 0.0)
        dweight = jnp.where(live, denv, 0.0)
        orders = (row8 + 1).astype(F32)
        angle = orders * jnp.minimum(u, 1.0)
        turns = jnp.floor(angle + 0.5)
        rest = angle - turns
        parity = turns * 0.5 - jnp.floor(turns * 0.5)
        sign = 1.0 - 4.0 * parity
        rest2 = rest * rest
        sine = sign * rest * polynomial(rest2, SIN)
        cosine = sign * polynomial(rest2, COS)
        radial = sine * inv
        dradial = (orders * (math.pi / CUT) * cosine - radial) * inv
        label = jnp.where(row8 < 2, own_label, near_label)
        hot = jnp.where(label == (row8 % 2).astype(F32), 1.0, 0.0)
        hot = jnp.where(row8 < 4, hot, 0.0)
        h1 = dot(wf_s[...], stack3(jnp.concatenate([radial, hot], axis=0)))
        slide = dot(wf_s[...], stack3(jnp.concatenate([dradial, jnp.zeros_like(hot)], axis=0)))
        t1 = jnp.tanh(h1)
        s1 = h1 + h1 * t1
        slope1 = (1.0 + t1) * (1.0 + (h1 - h1 * t1))
        edge = s1 * weight
        slide1[t] = dweight * s1 + weight * (slope1 * slide)
        weight_s[t] = weight
        dweight_s[t] = dweight
        unit_s[t] = vec * inv
        return weight, edge

    def first_row(x):
        found = [first(x, y) for y in range(TY)]
        env = in_row([over_edges(edge) for weight, edge in found]) * 0.25
        env = dot(w1b_s[...], stack3(env))
        states = []
        for y in range(TY):
            t = x * TY + y
            weight, edge = found[y]
            h2 = dot(w1a_s[...], stack3(edge)) + spread(of_tile(env, y))
            t2 = jnp.tanh(h2)
            s2 = h2 + h2 * t2
            silu2[t] = s2
            wslope2[t] = weight * ((0.5 + 0.5 * t2) * (1.0 + (h2 - h2 * t2)))
            second = edge + weight * s2
            second_s[t] = second
            states.append(over_edges(weight * second))
        qp = dot(w2bc_s[...], stack3(in_row(states) * 0.25))
        q_s[x] = qp[:CH]
        group = lane_group((16, LANES))
        for y in range(TY):
            sent = None
            for j in range(4):
                part = qp[CH + 16 * j : CH + 16 * j + 16]
                if j != y:
                    part = pltpu.roll(part, ((j - y) * 32) % LANES, 1)
                sent = part if j == 0 else jnp.where(group == j, part, sent)
            p_grid[1, 1 + x, 1 + y] = sent

    def row_of(i):
        return (3 * i) % 4

    def first_step(i, carry):
        x = row_of(i)
        first_row(x)
        for copy in outward_row(p_grid, sems, 26 + 8 * i, x):
            copy.start()

        @pl.when(i == 0)
        def _():
            for copy in outward_face(p_grid, sems, 58, -1):
                copy.start()

        @pl.when(i == 1)
        def _():
            for copy in outward_face(p_grid, sems, 67, 1):
                copy.start()

        return carry

    lax.fori_loop(0, TX, first_step, 0)

    def mix_step(i, carry):
        turned = []
        for v in range(4):
            t = i * 4 + v
            weight, dweight = weight_s[t], dweight_s[t]
            mix_s[t] = dot(w2a_s[...], stack3(second_s[t])) + spread(of_tile(q_s[i], v))
            first_slide = slide1[t]
            wslope = wslope2[t]
            moved = dot(w1a_s[...], stack3(first_slide))
            full = first_slide + dweight * silu2[t] + (2.0 * wslope) * moved
            slide2[t] = full
            slide_s[t] = weight * full + dweight * second_s[t]
            turned.append(over_edges(weight * wslope))
        m2_s[i] = in_row(turned)
        return carry

    lax.fori_loop(0, TILES // 4, mix_step, 0)
    for i in range(TX):
        for copy in outward_row(p_grid, sems, 26 + 8 * i, row_of(i)):
            copy.wait()
    for copy in outward_face(p_grid, sems, 58, -1):
        copy.wait()
    for copy in outward_face(p_grid, sems, 67, 1):
        copy.wait()

    def columns_step(px, carry):
        lanes16 = iota((16, LANES), 1) // 32
        for py in range(TY + 2):
            parts = [p_grid[z, px, py] for z in range(3)]
            for j in range(4):
                moved = [
                    parts[z] if z == j else pltpu.roll(parts[z], ((z - j) * 32) % LANES, 1)
                    for z in range(3)
                ]
                p_cols[px, py, 16 * j : 16 * j + 16, :] = jnp.where(
                    lanes16 == 0, moved[0], jnp.where(lanes16 == 1, moved[1], moved[2])
                )
        return carry

    lax.fori_loop(0, TX + 2, columns_step, 0)

    def third(x, y):
        t = x * TY + y
        near = jnp.concatenate([gather(p_cols, t, x, y, CH, m) for m in range(4)], axis=1)
        weight = weight_s[t]
        h3 = mix_s[t] + near
        t3 = jnp.tanh(h3)
        silu3[t] = h3 + h3 * t3
        slope3 = (0.5 + 0.5 * t3) * (1.0 + (h3 - h3 * t3))
        grad3 = (weight * weight) * spread(wo_s[...]) * slope3
        grad3_s[t] = grad3

    def gather_back(x, y):
        t = x * TY + y
        high, low = halves(grad3_s[t])
        added = dot_t(onehot[t], jnp.concatenate([high, low], axis=0))
        for c in range(9):
            px, py = x + c // 3, y + c % 3
            acc[px, py] = acc[px, py] + added[96 * c : 96 * c + 96]

    def fold(px):
        lanes16 = iota((16, LANES), 1)
        for py in range(TY + 2):
            for z in range(3):
                both = acc[px, py, 32 * z : 32 * z + 32, :]
                both = both + pltpu.roll(both, 64, 1)
                g_send[z, px, py] = jnp.where(lanes16 < 64, both[:16], both[16:])

    for y in range(TY):
        third(row_of(0), y)

    def third_step(i, carry):
        x = row_of(i)
        for y in range(TY):
            gather_back(x, y)
            third(row_of(i + 1), y)

        @pl.when(i == 0)
        def _():
            fold(0)
            for copy in homeward_face(g_send, g_recv, sems, 76, -1):
                copy.start()

        @pl.when(i == 1)
        def _():
            fold(TX + 1)
            for copy in homeward_face(g_send, g_recv, sems, 85, 1):
                copy.start()

        @pl.when(i == 2)
        def _():
            fold(TX)
            for copy in homeward_rows(g_send, g_recv, sems, 94, TX, 1):
                copy.start()

        return carry

    lax.fori_loop(0, TX - 1, third_step, 0)
    for y in range(TY):
        gather_back(row_of(TX - 1), y)
    for px in range(1, TX):
        fold(px)
    for copy in homeward_rows(g_send, g_recv, sems, 102, 1, TX - 1):
        copy.start()

    def back_step(i, carry):
        sums2, sums3 = [], []
        for v in range(4):
            t = i * 4 + v
            weight, dweight = weight_s[t], dweight_s[t]
            wo = spread(wo_s[...])
            ws3 = weight * silu3[t]
            out3 = second_s[t] + ws3
            energy = jnp.sum(over_edges(weight * out3) * wo_s[...], axis=0, keepdims=True)
            result_s[t] = energy
            grad3 = grad3_s[t]
            back = weight * wo + dot(w2at_s[...], stack3(grad3))
            direct_s[t] = jnp.sum(
                back * slide2[t] + (dweight * wo) * (out3 + ws3), axis=0, keepdims=True
            )
            sums2.append(over_edges(back * wslope2[t]))
            sums3.append(over_edges(grad3))
        sum2_s[i] = in_row(sums2)
        q_s[i] = dot(w2bt_s[...], stack3(in_row(sums3)))
        return carry

    lax.fori_loop(0, TILES // 4, back_step, 0)
    for copy in homeward_face(g_send, g_recv, sems, 76, -1):
        copy.wait()
    for copy in homeward_face(g_send, g_recv, sems, 85, 1):
        copy.wait()
    for copy in homeward_rows(g_send, g_recv, sems, 94, TX, 1):
        copy.wait()
    for copy in homeward_rows(g_send, g_recv, sems, 102, 1, TX - 1):
        copy.wait()

    for t in range(TILES):
        x, y = t // TY, t % TY
        total = g_send[1, 1 + x, 1 + y]
        for place in shares(x, y):
            total = total + g_recv[place]
        return_s[t] = total

    def last(t, dstate, denv):
        ddist = direct_s[t] + jnp.sum(
            spread(dstate) * slide_s[t] + spread(denv) * slide1[t], axis=0, keepdims=True
        )
        push = unit_s[t] * ddist
        own = over_edges(push)
        lane1 = iota((1, LANES), 1) // 32
        result_s[t] = jnp.where(
            lane1 == 0,
            own[0:1],
            jnp.where(lane1 == 1, own[1:2], jnp.where(lane1 == 2, own[2:3], result_s[t])),
        )
        o = o_s[t]
        b = b_s[t]
        at_o = iota((32, EDGES), 0) == o
        at_b = jnp.where(iota((32, EDGES), 0) == b, 1.0, 0.0).astype(BF16)
        pieces = []
        for c in range(3):
            pieces.extend(halves(push[c : c + 1]))
        tables = [
            jnp.where(at_o, jnp.broadcast_to(piece.astype(F32), (32, EDGES)), 0.0).astype(BF16)
            for piece in pieces
        ]
        spots = dot_t(jnp.concatenate(tables, axis=0), at_b)
        comps = [spots[64 * c : 64 * c + 32] + spots[64 * c + 32 : 64 * c + 64] for c in range(3)]
        f_tile[t] = jnp.concatenate(comps + [jnp.zeros((32, 32), F32)], axis=1)

    def last_step(i, carry):
        sums = [return_s[i * 4 + v] for v in range(4)]
        atoms = [half for total in sums for half in (total[:, :CH], total[:, CH:])]
        high, low = halves(jnp.concatenate(atoms, axis=0))
        wide = dot_t(w2ct_s[...], high)
        returned = (wide[:CH] + wide[CH:]) + dot_t(w2ct_s[:CH], low)
        dstate = (q_s[i] + returned) * 0.25
        denv = dot(w1bt_s[...], stack3(sum2_s[i] + dstate * m2_s[i])) * 0.25
        for v in range(4):
            last(i * 4 + v, of_tile(dstate, v), of_tile(denv, v))
        return carry

    lax.fori_loop(0, TILES // 4, last_step, 0)

    for px in range(TX + 2):
        for py in range(TY + 2):
            for z in range(3):
                total = None
                for c in range(9):
                    x, y = px - c // 3, py - c % 3
                    if 0 <= x < TX and 0 <= y < TY:
                        at = 3 * c + z
                        part = f_tile[x * TY + y, at : at + 1, :]
                        total = part if total is None else total + part
                f_send[z, px, py] = total

    copies = homeward(f_send, f_recv, sems, 110)
    for copy in copies:
        copy.start()
    for copy in copies:
        copy.wait()

    found = []
    for t in range(TILES):
        x, y = t // TY, t % TY
        total = f_send[1, 1 + x, 1 + y]
        for place in shares(x, y):
            total = total + f_recv[place]
        found.append(result_s[t] - total)
    rows, cols = iota((LANES, LANES), 0), iota((LANES, LANES), 1)
    place = jnp.where(rows == (cols % 4) * 32 + cols // 4, 1.0, 0.0).astype(F32)
    out_ref[...] = exact_dot(jnp.concatenate(found, axis=0), place)


def local(
    positions, species, counts, neighbours, w_radial, emb_center, emb_nbr, w_first, w_second, w_out
):
    tiles = (TX + 2, TY + 2)
    edges = pltpu.VMEM((TILES, CH, EDGES), F32)
    row = pltpu.VMEM((TILES, 1, EDGES), F32)
    entries = pltpu.VMEM((TILES, 1, EDGES), I32)
    rows = pltpu.VMEM((TX, CH, LANES), F32)
    wide = pltpu.VMEM((CH, 3 * CH), BF16)
    small_grid = pltpu.VMEM((3, *tiles, 1, LANES), F32)
    grid = pltpu.VMEM((3, *tiles, 16, LANES), F32)
    scratch = dict(
        pos_grid=small_grid,
        own_cols=pltpu.VMEM((TILES, 8, LANES), F32),
        pos_cols=pltpu.VMEM((*tiles, 8, LANES), F32),
        c9_s=entries,
        loc_s=entries,
        o_s=entries,
        b_s=entries,
        onehot=pltpu.VMEM((TILES, TARGETS, EDGES), BF16),
        wf_s=pltpu.VMEM((CH, 48), BF16),
        w1a_s=wide,
        w1b_s=wide,
        w2bc_s=pltpu.VMEM((2 * CH, 3 * CH), BF16),
        w2a_s=wide,
        w2at_s=wide,
        w2bt_s=wide,
        w2ct_s=pltpu.VMEM((2 * CH, CH), BF16),
        w1bt_s=wide,
        wo_s=pltpu.VMEM((CH, LANES), F32),
        silu2=edges,
        wslope2=edges,
        second_s=edges,
        slide1=edges,
        slide2=edges,
        slide_s=edges,
        mix_s=edges,
        silu3=edges,
        grad3_s=edges,
        weight_s=row,
        dweight_s=row,
        unit_s=pltpu.VMEM((TILES, 8, EDGES), F32),
        q_s=rows,
        m2_s=rows,
        sum2_s=rows,
        direct_s=row,
        return_s=pltpu.VMEM((TILES, 16, LANES), F32),
        p_grid=grid,
        p_cols=pltpu.VMEM((*tiles, CH, LANES), F32),
        acc=pltpu.VMEM((*tiles, 96, LANES), F32),
        g_send=grid,
        g_recv=grid,
        f_tile=pltpu.VMEM((TILES, 32, LANES), F32),
        f_send=small_grid,
        f_recv=small_grid,
        result_s=pltpu.VMEM((TILES, 1, LANES), F32),
        send_sem=pltpu.SemaphoreType.DMA((136,)),
        recv_sem=pltpu.SemaphoreType.DMA((136,)),
    )
    vmem = pl.BlockSpec(memory_space=pltpu.VMEM)
    out = pl.pallas_call(
        kernel,
        out_shape=jax.ShapeDtypeStruct((TILES, LANES), F32),
        in_specs=[vmem] * 10,
        out_specs=vmem,
        scratch_shapes=scratch,
        compiler_params=pltpu.CompilerParams(
            collective_id=0, has_side_effects=True, vmem_limit_bytes=60 * 2**20
        ),
        name="forces",
    )(
        positions.reshape(TILES, 3 * SLOTS),
        species.reshape(TILES, SLOTS),
        counts.transpose(0, 2, 1),
        neighbours.reshape(4 * TILES, LANES),
        w_radial.T,
        emb_center.T,
        emb_nbr.T,
        w_first,
        w_second,
        w_out.reshape(1, CH),
    )
    return out.reshape(TX, TY, 1, 4 * SLOTS)


def solution(mesh):
    tiled = P("gx", "gy", "gz", None)
    placed = (tiled, tiled, P("gx", "gy", "gz"), tiled, P(), P(), P(), P(), P(), P())
    return jax.shard_map(local, mesh=mesh, in_specs=placed, out_specs=tiled, check_vma=False)
```

```python
import math

import jax
import jax.numpy as jnp
from jax import lax
from jax.experimental import pallas as pl
from jax.experimental.pallas import tpu as pltpu
from jax.sharding import PartitionSpec as P

F32 = jnp.float32
BF16 = jnp.bfloat16
I32 = jnp.int32

CUT = 5.0
TILE = 8.0
CH = 64
NBR = 16
SLOTS = 32
EDGES = 512
TX = 4
TY = 4
TILES = TX * TY
LANES = 128
SPLIT = 5
TARGETS = SPLIT * 3 * SLOTS

DIRS = [
    (dx, dy, dz)
    for dz in (-1, 1, 0)
    for dx in (-1, 0, 1)
    for dy in (-1, 0, 1)
    if (dx, dy, dz) != (0, 0, 0)
]


def edge_of(step, count):
    if step == 0:
        return pl.ds(1, count)
    return pl.ds(count if step > 0 else 1, 1)


def ghost_of(step, count):
    if step == 0:
        return pl.ds(1, count)
    return pl.ds(count + 1 if step > 0 else 0, 1)


def device_at(step):
    names = ("gx", "gy", "gz")
    place = []
    for name, move in zip(names, step):
        size = lax.axis_size(name)
        place.append(lax.rem(lax.axis_index(name) + (move + size), size))
    return tuple(place)


def outward(buf, sems, base):
    send, recv = sems
    made = []
    for index, (dx, dy, dz) in enumerate(DIRS):
        made.append(
            pltpu.make_async_remote_copy(
                src_ref=buf.at[1, edge_of(dx, TX), edge_of(dy, TY)],
                dst_ref=buf.at[1 - dz, ghost_of(-dx, TX), ghost_of(-dy, TY)],
                send_sem=send.at[base + index],
                recv_sem=recv.at[base + index],
                device_id=device_at((dx, dy, dz)),
                device_id_type=pl.DeviceIdType.MESH,
            )
        )
    return made


FLAT = [(dy, dz) for dy in (0, -1, 1) for dz in (-1, 1, 0) if (dy, dz) != (0, 0)]
FACE = [(dy, dz) for dy in (-1, 0, 1) for dz in (-1, 1, 0)]


def remote(source, target, sems, index, step):
    send, recv = sems
    return pltpu.make_async_remote_copy(
        src_ref=source,
        dst_ref=target,
        send_sem=send.at[index],
        recv_sem=recv.at[index],
        device_id=device_at(step),
        device_id_type=pl.DeviceIdType.MESH,
    )


def outward_row(buf, sems, base, x):
    return [
        remote(
            buf.at[1, 1 + x, edge_of(dy, TY)],
            buf.at[1 - dz, 1 + x, ghost_of(-dy, TY)],
            sems,
            base + index,
            (0, dy, dz),
        )
        for index, (dy, dz) in enumerate(FLAT)
    ]


def outward_face(buf, sems, base, dx):
    x = TX if dx > 0 else 1
    return [
        remote(
            buf.at[1, x, edge_of(dy, TY)],
            buf.at[1 - dz, TX + 1 if dx < 0 else 0, ghost_of(-dy, TY)],
            sems,
            base + index,
            (dx, dy, dz),
        )
        for index, (dy, dz) in enumerate(FACE)
    ]


def homeward_rows(source, target, sems, base, px, count):
    made = []
    for index, (dy, dz) in enumerate(FLAT):
        place = (1 + dz, pl.ds(px, count), ghost_of(dy, TY))
        made.append(remote(source.at[place], target.at[place], sems, base + index, (0, dy, dz)))
    return made


def homeward_face(source, target, sems, base, dx):
    made = []
    for index, (dy, dz) in enumerate(FACE):
        place = (1 + dz, TX + 1 if dx > 0 else 0, ghost_of(dy, TY))
        made.append(remote(source.at[place], target.at[place], sems, base + index, (dx, dy, dz)))
    return made


def shares(x, y):
    found = []
    for dx, dy, dz in DIRS:
        if dx != 0 and x != (0 if dx > 0 else TX - 1):
            continue
        if dy != 0 and y != (0 if dy > 0 else TY - 1):
            continue
        px = x + 1 if dx == 0 else (TX + 1 if dx > 0 else 0)
        py = y + 1 if dy == 0 else (TY + 1 if dy > 0 else 0)
        found.append((1 + dz, px, py))
    return found


def halves(x):
    high = x.astype(BF16)
    low = (x - high.astype(F32)).astype(BF16)
    return high, low


def stack3(x):
    high, low = halves(x)
    return jnp.concatenate([high, low, high], axis=0)


def weight3(w):
    high, low = halves(w)
    return jnp.concatenate([high, high, low], axis=1)


def dot(left, right):
    return lax.dot_general(
        left, right, (((1,), (0,)), ((), ())), preferred_element_type=F32
    )


def dot_t(left, right):
    return lax.dot_general(
        left, right, (((1,), (1,)), ((), ())), preferred_element_type=F32
    )


def exact_dot(left, right):
    return lax.dot_general(
        left,
        right,
        (((1,), (0,)), ((), ())),
        preferred_element_type=F32,
        precision=lax.Precision.HIGHEST,
    )


def over_edges(x):
    total = (x[:, 0:128] + x[:, 128:256]) + (x[:, 256:384] + x[:, 384:512])
    total = total + pltpu.roll(total, 64, 1)
    return total + pltpu.roll(total, 32, 1)


def spread(x):
    return jnp.concatenate([x, x, x, x], axis=1)


def lane_group(shape):
    return iota(shape, 1) // 32


def in_row(tiles):
    group = lane_group(tiles[0].shape)
    total = tiles[0]
    for y in range(1, TY):
        total = jnp.where(group == y, tiles[y], total)
    return total


def of_tile(row, y):
    place = y * 32 + iota((8, LANES), 1) % 32
    parts = [
        jnp.take_along_axis(row[r : r + 8], place, axis=1) for r in range(0, row.shape[0], 8)
    ]
    return jnp.concatenate(parts, axis=0)


def polynomial(x, coefficients):
    total = jnp.full_like(x, coefficients[-1])
    for value in reversed(coefficients[:-1]):
        total = total * x + value
    return total


SIN = [(-1.0) ** i * math.pi ** (2 * i + 1) / math.factorial(2 * i + 1) for i in range(7)]
COS = [(-1.0) ** i * math.pi ** (2 * i) / math.factorial(2 * i) for i in range(8)]


def iota(shape, dim):
    return lax.broadcasted_iota(I32, shape, dim)


def kernel(
    pos_ref, spec_ref, count_ref, nbr_ref, wr_ref, ec_ref, en_ref, w1_ref, w2_ref, wo_ref,
    out_ref,
    pos_grid, own_cols, pos_cols, c9_s, loc_s, o_s, b_s,
    onehot, early_s, wf_s, w1a_s, w1b_s, w2bc_s, w2a_s, w2at_s, w2bt_s, w2ct_s, w1bt_s, wo_s,
    silu1, slope1, silu2, wslope2, second_s, slide1, slide2, slide_s, mix_s, silu3, grad3_s,
    weight_s, dweight_s, dradial_s, unit_s, q_s, m2_s, sum2_s, direct_s,
    p_grid, p_cols, acc, g_send, g_recv, f_tile, f_send, f_recv, result_s,
    send_sem, recv_sem,
):
    sems = (send_sem, recv_sem)
    barrier = pltpu.get_barrier_semaphore()
    for step in DIRS:
        pl.semaphore_signal(
            barrier, inc=1, device_id=device_at(step), device_id_type=pl.DeviceIdType.MESH
        )

    rows, cols = iota((96, LANES), 0), iota((96, LANES), 1)
    place = jnp.where(cols < 96, jnp.where(rows == (cols % 32) * 3 + cols // 32, 1.0, 0.0), 0.0)
    counts = []
    for x in range(TX):
        wide = jnp.broadcast_to(count_ref[x], (TY, TY))
        diagonal = jnp.where(iota((TY, TY), 0) == iota((TY, TY), 1), wide, 0)
        counts.append(jnp.sum(diagonal.astype(F32), axis=1, keepdims=True))
    count = jnp.concatenate(counts, axis=0).astype(I32)
    labels = jnp.where(iota((TILES, SLOTS), 1) < count, spec_ref[...], -1).astype(F32)
    shift = jnp.where(iota((SLOTS, LANES), 1) == iota((SLOTS, LANES), 0) + 96, 1.0, 0.0).astype(F32)
    packed = exact_dot(pos_ref[...], place) + exact_dot(labels, shift)
    for t in range(TILES):
        pos_grid[1, 1 + t // TY, 1 + t % TY] = packed[t : t + 1]

    pl.semaphore_wait(barrier, len(DIRS))
    copies = outward(pos_grid, sems, 0)
    for copy in copies:
        copy.start()

    half = 0.5
    table = jnp.concatenate([wr_ref[...], ec_ref[...], en_ref[...], jnp.zeros((4, CH), F32)], axis=0)
    wf_s[...] = weight3(table.T * half)
    w1 = w1_ref[...]
    w2 = w2_ref[...]
    w1a, w1b = w1[:, :CH], w1[:, CH:]
    w2a, w2b, w2c = w2[:, :CH], w2[:, CH : 2 * CH], w2[:, 2 * CH :]
    w1a_s[...] = weight3(w1a * half)
    w1b_s[...] = weight3(w1b * half)
    w2bc_s[...] = weight3(jnp.concatenate([w2b, w2c], axis=0) * half)
    w2a_s[...] = weight3(w2a * half)
    w2at_s[...] = weight3(w2a.T)
    w2bt_s[...] = weight3(w2b.T)
    w2ct_s[...] = jnp.concatenate(halves(w2c.T), axis=0)
    w1bt_s[...] = weight3(w1b.T)
    wo_s[...] = jnp.broadcast_to(
        jnp.broadcast_to(wo_ref[...], (8, CH)).T[:, 0:1], (CH, LANES)
    )

    entry = jnp.concatenate([nbr_ref[pl.ds(q, TILES, stride=4), :] for q in range(4)], axis=1)
    order = jnp.where(
        iota((EDGES, EDGES), 0) == (iota((EDGES, EDGES), 1) % 32) * 16 + iota((EDGES, EDGES), 1) // 32,
        1.0,
        0.0,
    ).astype(BF16)
    o_new = dot((entry // 32).astype(F32).astype(BF16), order).astype(I32)
    b_new = dot((entry % 32).astype(F32).astype(BF16), order).astype(I32)
    c9_new = o_new // 3
    loc_new = (o_new % 3) * 32 + b_new
    for t in range(TILES):
        o_s[t] = o_new[t : t + 1]
        b_s[t] = b_new[t : t + 1]
        c9_s[t] = c9_new[t : t + 1]
        loc_s[t] = loc_new[t : t + 1]

    def make_onehot(t, carry):
        c9 = c9_s[t]
        late = jnp.where(c9 >= SPLIT, 1, 0)
        early_s[t] = jnp.broadcast_to(1.0 - late.astype(F32), (16, EDGES)).astype(BF16)
        entry = (c9 - SPLIT * late) * 96 + loc_s[t]
        onehot[t] = jnp.where(iota((TARGETS, EDGES), 0) == entry, 1.0, 0.0).astype(BF16)
        return carry

    lax.fori_loop(0, TILES, make_onehot, 0)
    acc[...] = jnp.zeros_like(acc)

    for copy in copies:
        copy.wait()

    lane = iota((8, LANES), 1)
    sub = iota((8, LANES), 0)
    group = lane // 32
    pick = jnp.minimum(sub, 3) * 32 + lane % 32
    for px in range(TX + 2):
        for py in range(TY + 2):
            parts = []
            for z in range(3):
                row = jnp.broadcast_to(pos_grid[z, px, py], (8, LANES))
                parts.append(jnp.take_along_axis(row, pick, axis=1))
            pos_cols[px, py] = jnp.where(
                group == 0, parts[0], jnp.where(group == 1, parts[1], parts[2])
            )
            if 1 <= px <= TX and 1 <= py <= TY:
                own_cols[(px - 1) * TY + py - 1] = parts[1]

    def gather(columns, t, x, y, height, m):
        c9 = jnp.broadcast_to(c9_s[t, :, m * LANES : (m + 1) * LANES], (8, LANES))
        loc = jnp.broadcast_to(loc_s[t, :, m * LANES : (m + 1) * LANES], (8, LANES))
        outs = [None] * (height // 8)
        for c in range(9):
            for r in range(height // 8):
                source = columns[x + c // 3, y + c % 3, r * 8 : r * 8 + 8, :]
                got = jnp.take_along_axis(source, loc, axis=1)
                outs[r] = got if c == 0 else jnp.where(c9 == c, got, outs[r])
        return jnp.concatenate(outs, axis=0) if len(outs) > 1 else outs[0]

    def first(x, y):
        t = x * TY + y
        near = jnp.concatenate([gather(pos_cols, t, x, y, 8, m) for m in range(4)], axis=1)
        centre = spread(own_cols[t])
        o = o_s[t]
        ox = (o // 9 - 1).astype(F32) * TILE
        oy = (o // 3 % 3 - 1).astype(F32) * TILE
        oz = (o % 3 - 1).astype(F32) * TILE
        row8 = iota((8, EDGES), 0)
        move = jnp.where(row8 == 0, ox, jnp.where(row8 == 1, oy, jnp.where(row8 == 2, oz, 0.0)))
        vec = jnp.where(row8 < 3, (move + near) - centre, 0.0)
        dist = jnp.sqrt(jnp.sum(vec * vec, axis=0, keepdims=True))
        inv = 1.0 / dist
        u = dist * (1.0 / CUT)
        own_label = centre[3:4]
        near_label = near[3:4]
        live = (own_label >= 0.0) & (near_label >= 0.0) & (u < 1.0)
        u2 = u * u
        u5 = u2 * u2 * u
        env = 1.0 + u5 * u * (-28.0 + u * (48.0 - 21.0 * u))
        denv = (-168.0 / CUT) * u5 * ((1.0 - u) * (1.0 - u))
        weight = jnp.where(live, env, 0.0)
        dweight = jnp.where(live, denv, 0.0)
        orders = (row8 + 1).astype(F32)
        angle = orders * jnp.minimum(u, 1.0)
        turns = jnp.floor(angle + 0.5)
        rest = angle - turns
        parity = turns * 0.5 - jnp.floor(turns * 0.5)
        sign = 1.0 - 4.0 * parity
        rest2 = rest * rest
        sine = sign * rest * polynomial(rest2, SIN)
        cosine = sign * polynomial(rest2, COS)
        radial = sine * inv
        dradial = (orders * (math.pi / CUT) * cosine - radial) * inv
        label = jnp.where(row8 < 2, own_label, near_label)
        hot = jnp.where(label == (row8 % 2).astype(F32), 1.0, 0.0)
        hot = jnp.where(row8 < 4, hot, 0.0)
        h1 = dot(wf_s[...], stack3(jnp.concatenate([radial, hot], axis=0)))
        dradial_s[t] = dradial
        t1 = jnp.tanh(h1)
        s1 = h1 + h1 * t1
        silu1[t] = s1
        slope1[t] = (1.0 + t1) * (1.0 + (h1 - h1 * t1))
        edge = s1 * weight
        weight_s[t] = weight
        dweight_s[t] = dweight
        unit_s[t] = vec * inv
        return weight, edge

    def first_row(x):
        found = [first(x, y) for y in range(TY)]
        env = in_row([over_edges(edge) for weight, edge in found]) * 0.25
        env = dot(w1b_s[...], stack3(env))
        states = []
        for y in range(TY):
            t = x * TY + y
            weight, edge = found[y]
            h2 = dot(w1a_s[...], stack3(edge)) + spread(of_tile(env, y))
            t2 = jnp.tanh(h2)
            s2 = h2 + h2 * t2
            silu2[t] = s2
            wslope2[t] = weight * ((0.5 + 0.5 * t2) * (1.0 + (h2 - h2 * t2)))
            second = edge + weight * s2
            second_s[t] = second
            states.append(over_edges(weight * second))
        qp = dot(w2bc_s[...], stack3(in_row(states) * 0.25))
        q_s[x] = qp[:CH]
        group = lane_group((16, LANES))
        for y in range(TY):
            sent = None
            for j in range(4):
                part = qp[CH + 16 * j : CH + 16 * j + 16]
                if j != y:
                    part = pltpu.roll(part, ((j - y) * 32) % LANES, 1)
                sent = part if j == 0 else jnp.where(group == j, part, sent)
            p_grid[1, 1 + x, 1 + y] = sent

    def row_of(i):
        return (3 * i) % 4

    def first_step(i, carry):
        x = row_of(i)
        first_row(x)
        for copy in outward_row(p_grid, sems, 26 + 8 * i, x):
            copy.start()

        @pl.when(i == 0)
        def _():
            for copy in outward_face(p_grid, sems, 58, -1):
                copy.start()

        @pl.when(i == 1)
        def _():
            for copy in outward_face(p_grid, sems, 67, 1):
                copy.start()

        return carry

    lax.fori_loop(0, TX, first_step, 0)

    def mix_step(i, carry):
        turned = []
        for v in range(4):
            t = i * 4 + v
            weight, dweight = weight_s[t], dweight_s[t]
            mix_s[t] = dot(w2a_s[...], stack3(second_s[t])) + spread(of_tile(q_s[i], v))
            dradial = dradial_s[t]
            table = jnp.concatenate([dradial, jnp.zeros_like(dradial)], axis=0)
            first_slide = dweight * silu1[t] + weight * (slope1[t] * dot(wf_s[...], stack3(table)))
            slide1[t] = first_slide
            wslope = wslope2[t]
            moved = dot(w1a_s[...], stack3(first_slide))
            full = first_slide + dweight * silu2[t] + (2.0 * wslope) * moved
            slide2[t] = full
            slide_s[t] = weight * full + dweight * second_s[t]
            turned.append(over_edges(weight * wslope))
        m2_s[i] = in_row(turned)
        return carry

    lax.fori_loop(0, TILES // 4, mix_step, 0)
    for i in range(TX):
        for copy in outward_row(p_grid, sems, 26 + 8 * i, row_of(i)):
            copy.wait()
    for copy in outward_face(p_grid, sems, 58, -1):
        copy.wait()
    for copy in outward_face(p_grid, sems, 67, 1):
        copy.wait()

    def columns_step(px, carry):
        lanes16 = iota((16, LANES), 1) // 32
        for py in range(TY + 2):
            parts = [p_grid[z, px, py] for z in range(3)]
            for j in range(4):
                moved = [
                    parts[z] if z == j else pltpu.roll(parts[z], ((z - j) * 32) % LANES, 1)
                    for z in range(3)
                ]
                p_cols[px, py, 16 * j : 16 * j + 16, :] = jnp.where(
                    lanes16 == 0, moved[0], jnp.where(lanes16 == 1, moved[1], moved[2])
                )
        return carry

    lax.fori_loop(0, TX + 2, columns_step, 0)

    def third(x, y):
        t = x * TY + y
        near = jnp.concatenate([gather(p_cols, t, x, y, CH, m) for m in range(4)], axis=1)
        weight = weight_s[t]
        h3 = mix_s[t] + near
        t3 = jnp.tanh(h3)
        silu3[t] = h3 + h3 * t3
        slope3 = (0.5 + 0.5 * t3) * (1.0 + (h3 - h3 * t3))
        grad3 = (weight * weight) * spread(wo_s[...]) * slope3
        grad3_s[t] = grad3

    def gather_back(x, y):
        t = x * TY + y
        both = jnp.concatenate(halves(grad3_s[t]), axis=0)
        early = both * jnp.concatenate([early_s[t]] * 8, axis=0)
        added = dot_t(onehot[t], jnp.concatenate([early, both - early], axis=0))
        for c in range(9):
            px, py = x + c // 3, y + c % 3
            row, column = (c % SPLIT) * 96, (c // SPLIT) * LANES
            acc[px, py] = acc[px, py] + added[row : row + 96, column : column + LANES]

    def fold(px):
        lanes16 = iota((16, LANES), 1)
        for py in range(TY + 2):
            for z in range(3):
                both = acc[px, py, 32 * z : 32 * z + 32, :]
                both = both + pltpu.roll(both, 64, 1)
                g_send[z, px, py] = jnp.where(lanes16 < 64, both[:16], both[16:])

    for y in range(TY):
        third(row_of(0), y)

    def third_step(i, carry):
        x = row_of(i)
        for y in range(TY):
            gather_back(x, y)
            third(row_of(i + 1), y)

        @pl.when(i == 0)
        def _():
            fold(0)
            for copy in homeward_face(g_send, g_recv, sems, 76, -1):
                copy.start()

        @pl.when(i == 1)
        def _():
            fold(TX + 1)
            for copy in homeward_face(g_send, g_recv, sems, 85, 1):
                copy.start()

        @pl.when(i == 2)
        def _():
            fold(TX)
            for copy in homeward_rows(g_send, g_recv, sems, 94, TX, 1):
                copy.start()

        return carry

    lax.fori_loop(0, TX - 1, third_step, 0)
    for y in range(TY):
        gather_back(row_of(TX - 1), y)
    for px in range(1, TX):
        fold(px)
    for copy in homeward_rows(g_send, g_recv, sems, 102, 1, TX - 1):
        copy.start()

    def back_step(i, carry):
        sums2, sums3 = [], []
        for v in range(4):
            t = i * 4 + v
            weight, dweight = weight_s[t], dweight_s[t]
            wo = spread(wo_s[...])
            ws3 = weight * silu3[t]
            out3 = second_s[t] + ws3
            energy = jnp.sum(over_edges(weight * out3) * wo_s[...], axis=0, keepdims=True)
            result_s[t] = energy
            grad3 = grad3_s[t]
            back = weight * wo + dot(w2at_s[...], stack3(grad3))
            direct_s[t] = jnp.sum(
                back * slide2[t] + (dweight * wo) * (out3 + ws3), axis=0, keepdims=True
            )
            sums2.append(over_edges(back * wslope2[t]))
            sums3.append(over_edges(grad3))
        sum2_s[i] = in_row(sums2)
        q_s[i] = dot(w2bt_s[...], stack3(in_row(sums3)))
        return carry

    lax.fori_loop(0, TILES // 4, back_step, 0)
    for copy in homeward_face(g_send, g_recv, sems, 76, -1):
        copy.wait()
    for copy in homeward_face(g_send, g_recv, sems, 85, 1):
        copy.wait()
    for copy in homeward_rows(g_send, g_recv, sems, 94, TX, 1):
        copy.wait()
    for copy in homeward_rows(g_send, g_recv, sems, 102, 1, TX - 1):
        copy.wait()

    atoms = []
    for t in range(TILES):
        x, y = t // TY, t % TY
        total = g_send[1, 1 + x, 1 + y]
        for place in shares(x, y):
            total = total + g_recv[place]
        atoms.extend([total[:, :CH], total[:, CH:]])
    high, low = halves(jnp.concatenate(atoms, axis=0))
    wide = dot_t(w2ct_s[...], high)
    returned = (wide[:CH] + wide[CH:]) + dot_t(w2ct_s[:CH], low)
    dstates = [(q_s[x] + returned[:, x * LANES : (x + 1) * LANES]) * 0.25 for x in range(TX)]
    inner = [sum2_s[x] + dstates[x] * m2_s[x] for x in range(TX)]
    denvs = dot(w1bt_s[...], stack3(jnp.concatenate(inner, axis=1))) * 0.25
    for x in range(TX):
        q_s[x] = dstates[x]
        sum2_s[x] = denvs[:, x * LANES : (x + 1) * LANES]

    def push_row(x):
        dstate, denv = q_s[x], sum2_s[x]
        for y in range(TY):
            t = x * TY + y
            ddist = direct_s[t] + jnp.sum(
                spread(of_tile(dstate, y)) * slide_s[t] + spread(of_tile(denv, y)) * slide1[t],
                axis=0,
                keepdims=True,
            )
            unit_s[t] = unit_s[t] * ddist

    def last(t):
        push = unit_s[t]
        own = over_edges(push)
        lane1 = iota((1, LANES), 1) // 32
        result_s[t] = jnp.where(
            lane1 == 0,
            own[0:1],
            jnp.where(lane1 == 1, own[1:2], jnp.where(lane1 == 2, own[2:3], result_s[t])),
        )
        at_o = iota((32, EDGES), 0) == o_s[t]
        at_b = jnp.where(iota((32, EDGES), 0) == b_s[t], 1.0, 0.0).astype(BF16)
        pieces = []
        for c in range(3):
            pieces.extend(halves(push[c : c + 1]))
        tables = [
            jnp.where(at_o, jnp.broadcast_to(piece.astype(F32), (32, EDGES)), 0.0).astype(BF16)
            for piece in pieces
        ]
        spots = dot_t(jnp.concatenate(tables, axis=0), at_b)
        comps = [spots[64 * c : 64 * c + 32] + spots[64 * c + 32 : 64 * c + 64] for c in range(3)]
        f_tile[t] = jnp.concatenate(comps + [jnp.zeros((32, 32), F32)], axis=1)

    def force_sums(px):
        for py in range(TY + 2):
            for z in range(3):
                total = None
                for c in range(9):
                    x, y = px - c // 3, py - c % 3
                    if 0 <= x < TX and 0 <= y < TY:
                        at = 3 * c + z
                        part = f_tile[x * TY + y, at : at + 1, :]
                        total = part if total is None else total + part
                f_send[z, px, py] = total

    push_row(row_of(0))

    def last_step(i, carry):
        x = row_of(i)
        for y in range(TY):
            last(x * TY + y)
        push_row(row_of(i + 1))

        @pl.when(i == 0)
        def _():
            force_sums(0)
            for copy in homeward_face(f_send, f_recv, sems, 110, -1):
                copy.start()

        @pl.when(i == 1)
        def _():
            force_sums(TX + 1)
            for copy in homeward_face(f_send, f_recv, sems, 119, 1):
                copy.start()

        @pl.when(i == 2)
        def _():
            force_sums(TX)
            for copy in homeward_rows(f_send, f_recv, sems, 128, TX, 1):
                copy.start()

        return carry

    lax.fori_loop(0, TX - 1, last_step, 0)
    for y in range(TY):
        last(row_of(TX - 1) * TY + y)
    for px in range(1, TX):
        force_sums(px)
    for copy in homeward_rows(f_send, f_recv, sems, 136, 1, TX - 1):
        copy.start()

    for copy in homeward_face(f_send, f_recv, sems, 110, -1):
        copy.wait()
    for copy in homeward_face(f_send, f_recv, sems, 119, 1):
        copy.wait()
    for copy in homeward_rows(f_send, f_recv, sems, 128, TX, 1):
        copy.wait()
    for copy in homeward_rows(f_send, f_recv, sems, 136, 1, TX - 1):
        copy.wait()

    found = []
    for t in range(TILES):
        x, y = t // TY, t % TY
        total = f_send[1, 1 + x, 1 + y]
        for place in shares(x, y):
            total = total + f_recv[place]
        found.append(result_s[t] - total)
    rows, cols = iota((LANES, LANES), 0), iota((LANES, LANES), 1)
    place = jnp.where(rows == (cols % 4) * 32 + cols // 4, 1.0, 0.0).astype(F32)
    out_ref[...] = exact_dot(jnp.concatenate(found, axis=0), place)


def local(
    positions, species, counts, neighbours, w_radial, emb_center, emb_nbr, w_first, w_second, w_out
):
    tiles = (TX + 2, TY + 2)
    edges = pltpu.VMEM((TILES, CH, EDGES), F32)
    row = pltpu.VMEM((TILES, 1, EDGES), F32)
    entries = pltpu.VMEM((TILES, 1, EDGES), I32)
    rows = pltpu.VMEM((TX, CH, LANES), F32)
    wide = pltpu.VMEM((CH, 3 * CH), BF16)
    small_grid = pltpu.VMEM((3, *tiles, 1, LANES), F32)
    grid = pltpu.VMEM((3, *tiles, 16, LANES), F32)
    scratch = dict(
        pos_grid=small_grid,
        own_cols=pltpu.VMEM((TILES, 8, LANES), F32),
        pos_cols=pltpu.VMEM((*tiles, 8, LANES), F32),
        c9_s=entries,
        loc_s=entries,
        o_s=entries,
        b_s=entries,
        onehot=pltpu.VMEM((TILES, TARGETS, EDGES), BF16),
        early_s=pltpu.VMEM((TILES, 16, EDGES), BF16),
        wf_s=pltpu.VMEM((CH, 48), BF16),
        w1a_s=wide,
        w1b_s=wide,
        w2bc_s=pltpu.VMEM((2 * CH, 3 * CH), BF16),
        w2a_s=wide,
        w2at_s=wide,
        w2bt_s=wide,
        w2ct_s=pltpu.VMEM((2 * CH, CH), BF16),
        w1bt_s=wide,
        wo_s=pltpu.VMEM((CH, LANES), F32),
        silu1=edges,
        slope1=edges,
        silu2=edges,
        wslope2=edges,
        second_s=edges,
        slide1=edges,
        slide2=edges,
        slide_s=edges,
        mix_s=edges,
        silu3=edges,
        grad3_s=edges,
        weight_s=row,
        dweight_s=row,
        dradial_s=pltpu.VMEM((TILES, 8, EDGES), F32),
        unit_s=pltpu.VMEM((TILES, 8, EDGES), F32),
        q_s=rows,
        m2_s=rows,
        sum2_s=rows,
        direct_s=row,
        p_grid=grid,
        p_cols=pltpu.VMEM((*tiles, CH, LANES), F32),
        acc=pltpu.VMEM((*tiles, 96, LANES), F32),
        g_send=grid,
        g_recv=grid,
        f_tile=pltpu.VMEM((TILES, 32, LANES), F32),
        f_send=small_grid,
        f_recv=small_grid,
        result_s=pltpu.VMEM((TILES, 1, LANES), F32),
        send_sem=pltpu.SemaphoreType.DMA((144,)),
        recv_sem=pltpu.SemaphoreType.DMA((144,)),
    )
    vmem = pl.BlockSpec(memory_space=pltpu.VMEM)
    out = pl.pallas_call(
        kernel,
        out_shape=jax.ShapeDtypeStruct((TILES, LANES), F32),
        in_specs=[vmem] * 10,
        out_specs=vmem,
        scratch_shapes=scratch,
        compiler_params=pltpu.CompilerParams(
            collective_id=0, has_side_effects=True, vmem_limit_bytes=60 * 2**20
        ),
        name="forces",
    )(
        positions.reshape(TILES, 3 * SLOTS),
        species.reshape(TILES, SLOTS),
        counts.transpose(0, 2, 1),
        neighbours.reshape(4 * TILES, LANES),
        w_radial.T,
        emb_center.T,
        emb_nbr.T,
        w_first,
        w_second,
        w_out.reshape(1, CH),
    )
    return out.reshape(TX, TY, 1, 4 * SLOTS)


def solution(mesh):
    tiled = P("gx", "gy", "gz", None)
    placed = (tiled, tiled, P("gx", "gy", "gz"), tiled, P(), P(), P(), P(), P(), P())
    return jax.shard_map(local, mesh=mesh, in_specs=placed, out_specs=tiled, check_vma=False)
```
